128 devices in a mesh: seq: 128 (over z, x, y, core).
Axes of the slice: x: 4, y: 4, z: 4, core: 2. Of those that a mesh axis runs over, the one named last changes fastest.
Arguments:
- queries: bfloat16 [49152, 768], P('seq'), may hold values from -6 to 6
- keys: bfloat16 [49152, 768], P('seq'), may hold values from -6 to 6
- values: bfloat16 [49152, 768], P('seq'), may hold values from -6 to 6
- grad_out: bfloat16 [49152, 768], P('seq'), may hold values from -18 to 18
- offsets: int32 [3, 12], replicated, may hold values from 0 to 127, as said below
Outputs:
- attended: bfloat16 [49152, 768], P('seq')
- grad_queries: bfloat16 [49152, 768], P('seq')
- grad_keys: bfloat16 [49152, 768], P('seq')
- grad_values: bfloat16 [49152, 768], P('seq')
The draws below stay inside these ranges and needn't reach their ends.
Inputs may be any that keep to these rules, and one draw needn't show every extreme that they name: Row b of offsets holds the offsets of dilated branch b + 1; each entry is below that branch's dilation, and every row holds 0 and its dilation minus one.
All inputs are finite; a program needn't handle non-finite values.
Results may differ from the reference program's by a relative error of at most 0.0051.
Values may be sent and summed in bfloat16 or wider, within the bound.
No kernel may reach another device: no remote copies, remote signals or barrier semaphores. Data moves between devices by JAX's collectives and lax.ppermute only.
A program may use at most 128 MiB of HBM per device.

```python
import jax
import jax.numpy as jnp
from jax import lax

HEADS = 12
HEAD_DIM = 64
WIDTH = 768
TOK_DEV = 384
SPAN_NEAR = 4
SPAN_MID = 32
TOKENS = 49152
N_SEQ = 128


def offset_table(key):
    key = jax.random.fold_in(key, 5)
    run_lengths = (SPAN_NEAR, SPAN_MID, N_SEQ)
    row_list = []
    head_index = jnp.arange(HEADS)
    for branch in range(3):
        run_length = run_lengths[branch]
        draw_key, first_key, second_key = jax.random.split(jax.random.fold_in(key, branch), 3)
        picked = jax.random.randint(draw_key, (HEADS,), 0, run_length)
        low_head = jax.random.randint(first_key, (), 0, HEADS)
        high_head = (low_head + 1 + jax.random.randint(second_key, (), 0, HEADS - 1)) % HEADS
        picked = jnp.where(head_index == low_head, 0, picked)
        picked = jnp.where(head_index == high_head, run_length - 1, picked)
        row_list.append(picked)
    return jnp.stack(row_list).astype(jnp.int32)


def draw_queries(key, part):
    key = jax.random.fold_in(key, 11)
    first_key = jax.random.fold_in(key, 0)
    base = jnp.clip(0.3 * jax.random.normal(first_key, (TOKENS, WIDTH), jnp.float32), -6.0, 6.0)
    return base.astype(jnp.bfloat16)


def draw_keys(key, part):
    key = jax.random.fold_in(key, 23)
    first_key = jax.random.fold_in(key, 0)
    base = jnp.clip(2.3 * jax.random.normal(first_key, (TOKENS, WIDTH), jnp.float32), -6.0, 6.0)
    return base.astype(jnp.bfloat16)


def draw_grad_out(key, part):
    table = offset_table(key)
    key = jax.random.fold_in(key, 37)
    position = jnp.arange(TOKENS, dtype=jnp.int32) % N_SEQ
    taken = position[:, None] == table[2][None, :]
    boost = jnp.repeat(jnp.where(taken, 3.0, 1.0).astype(jnp.float32), HEAD_DIM, axis=1)
    base = jnp.clip(jax.random.normal(key, (TOKENS, WIDTH), jnp.float32), -6.0, 6.0)
    return (base * boost).astype(jnp.bfloat16)


def draw_offsets(key, part):
    return offset_table(key)


def levels(stream_key, shape, shards, low, largest):
    def one(dim, parts):
        steps = jax.random.uniform(jax.random.fold_in(jax.random.fold_in(stream_key, 6), dim), (parts,), jnp.float32, low / len(shards), largest / len(shards))
        return jnp.repeat(jnp.exp(steps), shape[dim] // parts).reshape((-1,) + (1,) * (len(shape) - dim - 1))

    factor_of = one(*shards[0])
    for cut in shards[1:]:
        factor_of = factor_of * one(*cut)
    return factor_of


def gaussian(own_key, shape, spread, bound, pieces=(), kind=jnp.bfloat16):
    drawn = jax.random.normal(own_key, shape, jnp.float32) * spread
    if len(pieces) > 0:
        drawn = levels(own_key, shape, pieces, -0.22, 0.18) * drawn
    return jnp.clip(drawn, min=-bound, max=bound).astype(kind)


def setup_inputs(seed: int = 0) -> dict:
    splits = jax.random.split(jax.random.key(seed), 6)
    queries = draw_queries(jax.random.fold_in(splits[5], 71), 0)
    keys = draw_keys(jax.random.fold_in(splits[5], 71), 0)
    values = gaussian(splits[2], (TOKENS, WIDTH), 1.0, 6.0, ((0, 128),))
    grad_out = draw_grad_out(jax.random.fold_in(splits[5], 71), 0)
    offsets = draw_offsets(jax.random.fold_in(splits[5], 71), 0)
    return dict(queries=queries, keys=keys, values=values, grad_out=grad_out, offsets=offsets)


SCALE = 0.125
NEGATIVE = -1.0e30


def select_rows(tensor, run_length, offset_row):
    shaped = tensor.reshape((tensor.shape[0] // run_length, run_length) + tensor.shape[1:])
    return shaped[:, offset_row, jnp.arange(HEADS)]


def spread_rows(blocks, run_length, offset_row, fill):
    base = jnp.full((blocks.shape[0], run_length) + blocks.shape[1:], fill, blocks.dtype)
    base = base.at[:, offset_row, jnp.arange(HEADS)].set(blocks)
    return base.reshape((blocks.shape[0] * run_length,) + blocks.shape[1:])


def segment_forward(operands):
    query_sel, key_sel, value_sel = operands
    scores = SCALE * jnp.einsum("ihd,jhd->hij", query_sel.astype(jnp.float32), key_sel.astype(jnp.float32))
    row_peak = jnp.max(scores, axis=2)
    weights = jnp.exp(scores - row_peak[:, :, None])
    row_total = jnp.sum(weights, axis=2)
    rounded = weights.astype(jnp.bfloat16).astype(jnp.float32)
    partial_value = jnp.einsum("hij,jhd->ihd", rounded, value_sel.astype(jnp.float32))
    return row_peak.T, row_total.T, partial_value


def segment_backward(operands):
    query_sel, key_sel, value_sel, grad_sel, lse_sel, delta_sel = operands
    query_wide = query_sel.astype(jnp.float32)
    key_wide = key_sel.astype(jnp.float32)
    grad_wide = grad_sel.astype(jnp.float32)
    scores = SCALE * jnp.einsum("ihd,jhd->hij", query_wide, key_wide)
    softmax = jnp.exp(scores - lse_sel.T[:, :, None])
    rounded = softmax.astype(jnp.bfloat16).astype(jnp.float32)
    grad_prob = jnp.einsum("ihd,jhd->hij", grad_wide, value_sel.astype(jnp.float32))
    grad_score = (softmax * (grad_prob - delta_sel.T[:, :, None])).astype(jnp.bfloat16).astype(jnp.float32)
    grad_query = SCALE * jnp.einsum("hij,jhd->ihd", grad_score, key_wide)
    grad_key = SCALE * jnp.einsum("hij,ihd->jhd", grad_score, query_wide)
    grad_value = jnp.einsum("hij,ihd->jhd", rounded, grad_wide)
    return grad_query, grad_key, grad_value


def reference(queries, keys, values, grad_out, offsets):
    shape_heads = (TOKENS, HEADS, HEAD_DIM)
    query_heads = queries.reshape(shape_heads)
    key_heads = keys.reshape(shape_heads)
    value_heads = values.reshape(shape_heads)
    grad_heads = grad_out.reshape(shape_heads)
    run_lengths = (1, SPAN_NEAR, SPAN_MID, N_SEQ)
    offset_rows = jnp.concatenate([jnp.zeros((1, HEADS), jnp.int32), offsets.astype(jnp.int32)], axis=0)
    peak_list = []
    total_list = []
    partial_list = []
    for branch in range(4):
        run_length = run_lengths[branch]
        segment_count = N_SEQ // run_length
        offset_row = offset_rows[branch]

        def in_segments(tensor):
            picked = select_rows(tensor, run_length, offset_row)
            return picked.reshape((segment_count, TOK_DEV) + picked.shape[1:])

        row_peak, row_total, partial_value = lax.map(segment_forward, (in_segments(query_heads), in_segments(key_heads), in_segments(value_heads)))
        flat = TOKENS // run_length
        peak_list.append(spread_rows(row_peak.reshape(flat, HEADS), run_length, offset_row, NEGATIVE))
        total_list.append(spread_rows(row_total.reshape(flat, HEADS), run_length, offset_row, 0.0))
        partial_list.append(spread_rows(partial_value.reshape(flat, HEADS, HEAD_DIM), run_length, offset_row, 0.0))
    peaks = jnp.stack(peak_list)
    best = jnp.max(peaks, axis=0)
    denominator = jnp.sum(jnp.stack(total_list) * jnp.exp(peaks - best[None]), axis=0)
    log_total = best + jnp.log(denominator)
    combined = jnp.sum(jnp.exp(peaks - log_total[None])[..., None] * jnp.stack(partial_list), axis=0)
    attended = combined.astype(jnp.bfloat16)
    delta = jnp.sum(grad_heads.astype(jnp.float32) * attended.astype(jnp.float32), axis=2)
    grad_query_sum = jnp.zeros(shape_heads, jnp.float32)
    grad_key_sum = jnp.zeros(shape_heads, jnp.float32)
    grad_value_sum = jnp.zeros(shape_heads, jnp.float32)
    for branch in range(4):
        run_length = run_lengths[branch]
        segment_count = N_SEQ // run_length
        offset_row = offset_rows[branch]

        def in_segments(tensor):
            picked = select_rows(tensor, run_length, offset_row)
            return picked.reshape((segment_count, TOK_DEV) + picked.shape[1:])

        grad_query, grad_key, grad_value = lax.map(segment_backward, (in_segments(query_heads), in_segments(key_heads), in_segments(value_heads), in_segments(grad_heads), in_segments(log_total), in_segments(delta)))
        flat = (TOKENS // run_length, HEADS, HEAD_DIM)
        grad_query_sum = grad_query_sum + spread_rows(grad_query.reshape(flat), run_length, offset_row, 0.0)
        grad_key_sum = grad_key_sum + spread_rows(grad_key.reshape(flat), run_length, offset_row, 0.0)
        grad_value_sum = grad_value_sum + spread_rows(grad_value.reshape(flat), run_length, offset_row, 0.0)
    out_shape = (TOKENS, WIDTH)
    return (attended.reshape(out_shape), grad_query_sum.reshape(out_shape).astype(jnp.bfloat16), grad_key_sum.reshape(out_shape).astype(jnp.bfloat16), grad_value_sum.reshape(out_shape).astype(jnp.bfloat16))
```

```python
import jax
import jax.numpy as jnp
from jax import lax
from jax.experimental import pallas as pl
from jax.experimental.pallas import tpu as pltpu
from jax.sharding import PartitionSpec as P

HEADS = 12
HEAD_DIM = 64
PAIRS = 6
LANES = 128
WIDTH = 768
TOK = 384
SPAN_NEAR = 4
SPAN_MID = 32
SPAN_ALL = 128
SPANS = (SPAN_NEAR, SPAN_MID, SPAN_ALL)
NEAR = TOK // SPAN_NEAR
MID = TOK // SPAN_MID
FAR = TOK // SPAN_ALL
MID_SLOT = 2 * MID
FAR_SLOT = 8
CHIPS = 64
PLANE = 16
SCALE = 0.125
NEGATIVE = -1e30
F32 = jnp.float32
BF16 = jnp.bfloat16
EXACT = lax.Precision.HIGHEST


def iota(shape, axis):
    return lax.broadcasted_iota(jnp.int32, shape, axis)


def nt(a, b):
    return lax.dot_general(a, b, (((1,), (1,)), ((), ())), preferred_element_type=F32)


def nn(a, b):
    return lax.dot_general(a, b, (((1,), (0,)), ((), ())), preferred_element_type=F32)


def tn(a, b):
    return lax.dot_general(a, b, (((0,), (0,)), ((), ())), preferred_element_type=F32)


def exact_nn(a, b):
    return lax.dot_general(
        a, b, (((1,), (0,)), ((), ())), precision=EXACT, preferred_element_type=F32
    )


def one_hot(test):
    return jnp.where(test, 1.0, 0.0).astype(F32)


def halves(x):
    hi = x.astype(BF16)
    return hi, (x - hi.astype(F32)).astype(BF16)


def offset_row(offsets_ref, branch):
    head = iota((1, WIDTH), 1) // HEAD_DIM
    row = jnp.zeros((1, WIDTH), jnp.int32)
    for h in range(HEADS):
        row = jnp.where(head == h, offsets_ref[branch, h], row)
    return row


def offset_column(offsets_ref, branch):
    head = iota((16, 1), 0)
    column = jnp.zeros((16, 1), jnp.int32)
    for h in range(HEADS):
        column = jnp.where(head == h, offsets_ref[branch, h], column)
    return column


def pair_block(x):
    lane = iota(x.shape, 1)
    zero = jnp.zeros((), x.dtype)
    return jnp.concatenate(
        [jnp.where(lane < HEAD_DIM, x, zero), jnp.where(lane >= HEAD_DIM, x, zero)], axis=0
    )


def head_block(x, slots):
    tall = jnp.concatenate([x] * HEADS, axis=0)
    own = iota(tall.shape, 1) // HEAD_DIM == iota(tall.shape, 0) // slots
    return jnp.where(own, tall, 0.0)


def head_sum(x, slots):
    own = iota(x.shape, 1) // HEAD_DIM == iota(x.shape, 0) // slots
    return jnp.sum(jnp.where(own, x, 0.0).reshape(HEADS, slots, WIDTH), axis=0)


def stat_up(row, slots, span):
    count = row.shape[1]
    wide = jnp.where(iota((16, count), 1) // slots == iota((16, count), 0), row, 0.0)
    up = one_hot(iota((count, TOK), 0) % slots == iota((count, TOK), 1) // span)
    return exact_nn(wide, up)


def stat_down(x, slots, span):
    count = HEADS * slots
    down = one_hot(iota((TOK, count), 0) // span == iota((TOK, count), 1) % slots)
    wide = exact_nn(x, down)
    keep = iota((16, count), 1) // slots == iota((16, count), 0)
    return jnp.sum(jnp.where(keep, wide, 0.0), axis=0, keepdims=True)


def spread_t(x, slots, span):
    hi, lo = halves(x)
    up = one_hot(iota((slots, TOK), 0) == iota((slots, TOK), 1) // span).astype(BF16)
    return tn(hi, up) + tn(lo, up)


def spread_tok(x, slots, span):
    hi, lo = halves(x)
    up = one_hot(iota((TOK, slots), 1) == iota((TOK, slots), 0) // span).astype(BF16)
    return nn(up, hi) + nn(up, lo)


def spread_near_t(x):
    hi, lo = halves(x)
    up = one_hot(iota((LANES, TOK), 0) == iota((LANES, TOK), 1) // SPAN_NEAR).astype(BF16)
    return nn(hi, up) + nn(lo, up)


def call(body, out_shape, scratch=(), n_in=0, smem=(0,), cost=5):
    specs = []
    for i in range(n_in):
        specs.append(
            pl.BlockSpec(memory_space=pltpu.SMEM)
            if i in smem
            else pl.BlockSpec(memory_space=pltpu.VMEM)
        )
    many = isinstance(out_shape, (list, tuple))
    return pl.pallas_call(
        body,
        out_shape=out_shape,
        in_specs=specs,
        out_specs=[pl.BlockSpec(memory_space=pltpu.VMEM)] * len(out_shape)
        if many
        else pl.BlockSpec(memory_space=pltpu.VMEM),
        scratch_shapes=list(scratch),
        compiler_params=pltpu.CompilerParams(vmem_limit_bytes=56 * 1024 * 1024),
        cost_estimate=pl.CostEstimate(
            flops=cost * 1000000000, bytes_accessed=cost * 3000000, transcendentals=0
        ),
    )


def shape(rows, cols, dtype):
    return jax.ShapeDtypeStruct((rows, cols), dtype)


def select_body(off, q, k, v, g, near_kv, near_qg, mid_kvqg, far_kv, far_qg, own, wide, tmp):
    for a, ref in enumerate((k, v, q, g)):
        for p in range(PAIRS):
            base = (a * PAIRS + p) * TOK
            wide[base : base + TOK, :] = ref[:, p * LANES : (p + 1) * LANES].astype(F32)
    first = iota((1, LANES), 1) < HEAD_DIM
    tmp[...] = jnp.zeros((64, WIDTH), F32)
    far = iota((8, LANES), 0)
    for a in range(4):
        near_ref, near_row = (near_kv, a * NEAR) if a < 2 else (near_qg, (a - 2) * NEAR)
        for p in range(PAIRS):
            lanes = slice(p * LANES, (p + 1) * LANES)
            h = 2 * p
            base = (a * PAIRS + p) * TOK
            a0 = wide[pl.ds(base + off[0, h], NEAR, stride=SPAN_NEAR), :]
            a1 = wide[pl.ds(base + off[0, h + 1], NEAR, stride=SPAN_NEAR), :]
            near_ref[near_row : near_row + NEAR, lanes] = jnp.where(first, a0, a1).astype(BF16)
            for i in range(MID):
                b0 = wide[pl.ds(base + off[1, h] + i * SPAN_MID, 1), :]
                b1 = wide[pl.ds(base + off[1, h + 1] + i * SPAN_MID, 1), :]
                tmp[a * MID + i : a * MID + i + 1, lanes] = jnp.where(first, b0, b1)
            for i in range(FAR):
                c0 = wide[pl.ds(base + off[2, h] + i * SPAN_ALL, 1), :]
                c1 = wide[pl.ds(base + off[2, h + 1] + i * SPAN_ALL, 1), :]
                tmp[48 + a * FAR + i : 48 + a * FAR + i + 1, lanes] = jnp.where(first, c0, c1)
    mid = tmp[0:48, :]
    mid16 = mid.astype(BF16)
    for d in range(PLANE):
        mid_kvqg[d * 48 : (d + 1) * 48, :] = mid16
    far_rows = tmp[48:64, :]
    kv3 = far_rows[0:8]
    valid = iota((8, WIDTH), 0) < 2 * FAR
    kv8 = jnp.where(valid, kv3, 0.0)
    kv16 = jnp.concatenate([kv8, kv8], axis=0).astype(BF16)
    for d in range(CHIPS // 2):
        far_kv[d * 16 : (d + 1) * 16, :] = kv16
    far_qg[...] = jnp.concatenate([jnp.where(valid, tmp[54:62, :], 0.0)] * 2, axis=0).astype(BF16)
    row = iota((16, WIDTH), 0)
    for a in range(4):
        own[a * 16 : (a + 1) * 16, :] = jnp.where(
            row < MID, tmp[a * MID : a * MID + 16, :], 0.0
        ).astype(BF16)
        part = tmp[48 + a * FAR : 48 + a * FAR + 3, :]
        part = jnp.concatenate([part, jnp.zeros((13, WIDTH), F32)], axis=0)
        own[64 + a * 16 : 64 + (a + 1) * 16, :] = part.astype(BF16)


def local_forward_body(q, k, v, out_t, peak, total):
    peak[...] = jnp.zeros((16, TOK), F32)
    total[...] = jnp.ones((16, TOK), F32)
    for p in range(PAIRS):
        lanes = slice(p * LANES, (p + 1) * LANES)
        s = SCALE * nt(k[:, lanes], pair_block(q[:, lanes]))
        m = jnp.max(s, axis=0, keepdims=True)
        w = jnp.exp(s - m)
        t = jnp.sum(w, axis=0, keepdims=True)
        o = tn(v[:, lanes], w.astype(BF16))
        for e in range(2):
            cols = slice(e * TOK, (e + 1) * TOK)
            rows = slice(p * LANES + e * HEAD_DIM, p * LANES + (e + 1) * HEAD_DIM)
            out_t[rows, :] = o[e * HEAD_DIM : (e + 1) * HEAD_DIM, cols]
            peak[2 * p + e : 2 * p + e + 1, :] = m[:, cols]
            total[2 * p + e : 2 * p + e + 1, :] = t[:, cols]


def near_pair(refs, part, lanes):
    return jnp.concatenate([r[part * NEAR : (part + 1) * NEAR, lanes] for r in refs], axis=0)


def near_queries(ref, part, lanes):
    x = ref[part * NEAR : (part + 1) * NEAR, lanes]
    return pair_block(jnp.concatenate([x, jnp.zeros((LANES - NEAR, LANES), x.dtype)], axis=0))


def near_forward_body(qg, kv0, kv1, kv2, kv3, out_t, peak, total):
    refs = (kv0, kv1, kv2, kv3)
    peak[...] = jnp.zeros((16, LANES), F32)
    total[...] = jnp.ones((16, LANES), F32)
    for p in range(PAIRS):
        lanes = slice(p * LANES, (p + 1) * LANES)
        s = SCALE * nt(near_pair(refs, 0, lanes), near_queries(qg, 0, lanes))
        m = jnp.max(s, axis=0, keepdims=True)
        w = jnp.exp(s - m)
        t = jnp.sum(w, axis=0, keepdims=True)
        o = tn(near_pair(refs, 1, lanes), w.astype(BF16))
        for e in range(2):
            cols = slice(e * LANES, (e + 1) * LANES)
            rows = slice(p * LANES + e * HEAD_DIM, p * LANES + (e + 1) * HEAD_DIM)
            out_t[rows, :] = o[e * HEAD_DIM : (e + 1) * HEAD_DIM, cols]
            peak[2 * p + e : 2 * p + e + 1, :] = m[:, cols]
            total[2 * p + e : 2 * p + e + 1, :] = t[:, cols]


def far_forward(kv, query, slots, slot_rows, count):
    s = SCALE * nt(kv, head_block(query, slots).astype(BF16))
    valid = iota(s.shape, 0) % slot_rows < count
    s = jnp.where(valid, s, NEGATIVE)
    m = jnp.max(s, axis=0, keepdims=True)
    w = jnp.exp(s - m)
    t = jnp.sum(w, axis=0, keepdims=True)
    o = tn(pltpu.roll(w, count, 0).astype(BF16), kv)
    return m, t, head_sum(o, slots)


def merge_body(
    off, g, out0, peak0, total0, out1, peak1, total1, mid_a, mid_b, far_a, far_b, own, far_qg,
    attended, lse_ref, delta_ref, near_stat, far_send,
):
    mid = jnp.concatenate([mid_a[...], mid_b[...]], axis=0)
    far = jnp.concatenate([far_a[...], far_b[...]], axis=0)
    m2, t2, o2 = far_forward(mid, own[32:48, :].astype(F32), 16, 48, MID)
    m3, t3, o3 = far_forward(far, own[96:112, :].astype(F32)[0:8], 8, FAR_SLOT, FAR)
    token = iota((16, TOK), 1)
    taken = [token % SPANS[b] == offset_column(off, b) for b in range(3)]
    up1 = one_hot(iota((LANES, TOK), 0) == iota((LANES, TOK), 1) // SPAN_NEAR)
    peaks = [exact_nn(peak1[...], up1), stat_up(m2, 16, SPAN_MID), stat_up(m3, 8, SPAN_ALL)]
    totals = [exact_nn(total1[...], up1), stat_up(t2, 16, SPAN_MID), stat_up(t3, 8, SPAN_ALL)]
    peaks = [jnp.where(t, x, NEGATIVE) for t, x in zip(taken, peaks)]
    best = peak0[...]
    for x in peaks:
        best = jnp.maximum(best, x)
    den = total0[...] * jnp.exp(peak0[...] - best)
    for x, y, t in zip(peaks, totals, taken):
        den = den + jnp.where(t, y * jnp.exp(x - best), 0.0)
    lse = best + jnp.log(den)
    weight0 = jnp.exp(peak0[...] - lse)
    weights = [jnp.where(t, jnp.exp(x - lse), 0.0) for x, t in zip(peaks, taken)]
    s1 = spread_near_t(out1[...])
    s2 = spread_t(o2, 16, SPAN_MID)
    s3 = spread_t(o3, 8, SPAN_ALL)
    parts = []
    for h in range(HEADS):
        rows = slice(h * HEAD_DIM, (h + 1) * HEAD_DIM)
        one = slice(h, h + 1)
        parts.append(
            out0[rows, :] * weight0[one]
            + s1[rows] * weights[0][one]
            + s2[rows] * weights[1][one]
            + s3[rows] * weights[2][one]
        )
    att = jnp.concatenate(parts, axis=0).T.astype(BF16)
    attended[...] = att
    hi, lo = halves(g[...].astype(F32) * att.astype(F32))
    pick = one_hot(iota((16, WIDTH), 1) // HEAD_DIM == iota((16, WIDTH), 0)).astype(BF16)
    delta = nt(pick, hi) + nt(pick, lo)
    lse_ref[...] = lse
    delta_ref[...] = delta
    down1 = one_hot(iota((TOK, LANES), 1) == iota((TOK, LANES), 0) // SPAN_NEAR)
    near_stat[0:16, :] = exact_nn(jnp.where(taken[0], lse, 0.0), down1)
    near_stat[16:32, :] = exact_nn(jnp.where(taken[0], delta, 0.0), down1)
    column = iota((TOK, 256), 1) % 16
    row = iota((TOK, 256), 0)
    down2 = one_hot(row // SPAN_MID == column)
    down3 = one_hot(row // SPAN_ALL + MID == column)
    keep = iota((16, 256), 1) // 16 == iota((16, 256), 0)
    lines = []
    for x in (lse, delta):
        wide = exact_nn(jnp.where(taken[1], x, 0.0), down2) + exact_nn(
            jnp.where(taken[2], x, 0.0), down3
        )
        line = jnp.sum(jnp.where(keep, wide, 0.0), axis=0, keepdims=True)
        first = line.astype(BF16).astype(F32)
        second = (line - first).astype(BF16).astype(F32)
        third = line - first - second
        lines.append(jnp.concatenate([first, second, third], axis=1))
    r = iota((16, WIDTH), 0) % 8
    send = jnp.where(r == 6, lines[0], jnp.where(r == 7, lines[1], far_qg[...].astype(F32)))
    send = send.astype(BF16)
    for d in range(CHIPS // 2):
        far_send[d * 16 : (d + 1) * 16, :] = send


def local_backward_body(q, k, v, g, lse, delta, dq_t, dk, dv):
    for p in range(PAIRS):
        lanes = slice(p * LANES, (p + 1) * LANES)
        qb = pair_block(q[:, lanes])
        gb = pair_block(g[:, lanes])
        lr = jnp.concatenate([lse[2 * p : 2 * p + 1, :], lse[2 * p + 1 : 2 * p + 2, :]], axis=1)
        dr = jnp.concatenate([delta[2 * p : 2 * p + 1, :], delta[2 * p + 1 : 2 * p + 2, :]], axis=1)
        prob = jnp.exp(SCALE * nt(k[:, lanes], qb) - lr)
        ds = (prob * (nt(v[:, lanes], gb) - dr)).astype(BF16)
        dv[:, lanes] = nn(prob.astype(BF16), gb)
        dk[:, lanes] = SCALE * nn(ds, qb)
        dq = SCALE * tn(k[:, lanes], ds)
        for e in range(2):
            rows = slice(p * LANES + e * HEAD_DIM, p * LANES + (e + 1) * HEAD_DIM)
            dq_t[rows, :] = dq[e * HEAD_DIM : (e + 1) * HEAD_DIM, e * TOK : (e + 1) * TOK]


def far_query_grad(kv, query, grad, lse, delta, slots, slot_rows, count):
    s = SCALE * nt(kv, head_block(query, slots).astype(BF16))
    valid = iota(s.shape, 0) % slot_rows < count
    prob = jnp.exp(jnp.where(valid, s - lse, NEGATIVE))
    dp = nt(kv, head_block(grad, slots).astype(BF16))
    dp = pltpu.roll(dp, dp.shape[0] - count, 0)
    ds = jnp.where(valid, prob * (dp - delta), 0.0).astype(BF16)
    return SCALE * head_sum(tn(ds, kv), slots)


def query_grad_body(
    off, qg, kv0, kv1, kv2, kv3, mid_a, mid_b, far_a, far_b, own, lse, delta, near_stat, dq_t,
    grad_q, near_t,
):
    refs = (kv0, kv1, kv2, kv3)
    for p in range(PAIRS):
        lanes = slice(p * LANES, (p + 1) * LANES)
        h = 2 * p
        lr = jnp.concatenate([near_stat[h : h + 1, :], near_stat[h + 1 : h + 2, :]], axis=1)
        dr = jnp.concatenate([near_stat[16 + h : 17 + h, :], near_stat[17 + h : 18 + h, :]], axis=1)
        keys = near_pair(refs, 0, lanes)
        prob = jnp.exp(SCALE * nt(keys, near_queries(qg, 0, lanes)) - lr)
        dp = nt(near_pair(refs, 1, lanes), near_queries(qg, 1, lanes))
        ds = (prob * (dp - dr)).astype(BF16)
        dq = SCALE * tn(keys, ds)
        for e in range(2):
            rows = slice(p * LANES + e * HEAD_DIM, p * LANES + (e + 1) * HEAD_DIM)
            near_t[rows, :] = dq[e * HEAD_DIM : (e + 1) * HEAD_DIM, e * LANES : (e + 1) * LANES]
    token = iota((16, TOK), 1)
    taken = [token % SPANS[b] == offset_column(off, b) for b in range(3)]
    mid = jnp.concatenate([mid_a[...], mid_b[...]], axis=0)
    far = jnp.concatenate([far_a[...], far_b[...]], axis=0)
    down = []
    for b, slots in ((1, 16), (2, 8)):
        for x in (lse, delta):
            down.append(stat_down(jnp.where(taken[b], x[...], 0.0), slots, SPANS[b]))
    dq2 = far_query_grad(
        mid, own[32:48, :].astype(F32), own[48:64, :].astype(F32), down[0], down[1], 16, 48, MID
    )
    dq3 = far_query_grad(
        far, own[96:112, :].astype(F32)[0:8], own[112:128, :].astype(F32)[0:8],
        down[2], down[3], 8, FAR_SLOT, FAR,
    )
    s1 = spread_near_t(near_t[...])
    s2 = spread_t(dq2, 16, SPAN_MID)
    s3 = spread_t(dq3, 8, SPAN_ALL)
    parts = []
    for h in range(HEADS):
        rows = slice(h * HEAD_DIM, (h + 1) * HEAD_DIM)
        total = dq_t[rows, :]
        for t, s in zip(taken, (s1, s2, s3)):
            total = total + jnp.where(t[h : h + 1], s[rows], 0.0)
        parts.append(total)
    grad_q[...] = jnp.concatenate(parts, axis=0).T.astype(BF16)


def near_key_body(kv, qg0, qg1, qg2, qg3, st0, st1, st2, st3, dk_out, dv_out):
    for p in range(PAIRS):
        lanes = slice(p * LANES, (p + 1) * LANES)
        kb = pair_block(kv[0:NEAR, lanes])
        vb = pair_block(kv[NEAR : 2 * NEAR, lanes])
        head = iota((2 * NEAR, NEAR), 0) < NEAR
        dk = jnp.zeros((2 * NEAR, LANES), F32)
        dv = jnp.zeros((2 * NEAR, LANES), F32)
        for qg, st in ((qg0, st0), (qg1, st1), (qg2, st2), (qg3, st3)):
            h = 2 * p
            queries = qg[0:NEAR, lanes]
            grads = qg[NEAR : 2 * NEAR, lanes]
            lr = jnp.where(head, st[h : h + 1, 0:NEAR], st[h + 1 : h + 2, 0:NEAR])
            dr = jnp.where(head, st[16 + h : 17 + h, 0:NEAR], st[17 + h : 18 + h, 0:NEAR])
            prob = jnp.exp(SCALE * nt(kb, queries) - lr)
            ds = (prob * (nt(vb, grads) - dr)).astype(BF16)
            dk = dk + nn(ds, queries)
            dv = dv + nn(prob.astype(BF16), grads)
        first = iota((NEAR, LANES), 1) < HEAD_DIM
        dk_out[:, lanes] = SCALE * jnp.where(first, dk[0:NEAR], dk[NEAR:])
        dv_out[:, lanes] = jnp.where(first, dv[0:NEAR], dv[NEAR:])


def stat_expand(line, rows, slot_rows, first, count, slots):
    devices = line.shape[0]
    x = jnp.broadcast_to(line[:, None, :], (devices, slot_rows, WIDTH)).reshape(rows, WIDTH)
    slot = iota((rows, WIDTH), 0) % slot_rows
    x = jnp.where((iota((rows, WIDTH), 1) % 16 == slot + first) & (slot < count), x, 0.0)
    columns = HEADS * slots
    pick = one_hot(
        iota((WIDTH, columns), 0) % 256 // 16 == iota((WIDTH, columns), 1) // slots
    ).astype(BF16)
    return nn(x.astype(BF16), pick)


def far_key_grad(qg, key, value, lse, delta, slots, slot_rows, count, base):
    rows = qg.shape[0]
    s = SCALE * nt(qg, head_block(key, slots).astype(BF16))
    slot = iota(s.shape, 0) % slot_rows
    valid = (slot >= base) & (slot < base + count)
    prob = jnp.exp(jnp.where(valid, s - lse, NEGATIVE))
    dp = nt(qg, head_block(value, slots).astype(BF16))
    dp = pltpu.roll(dp, rows - count, 0)
    ds = jnp.where(valid, prob * (dp - delta), 0.0).astype(BF16)
    dk = SCALE * head_sum(tn(ds, qg), slots)
    dv = head_sum(tn(pltpu.roll(prob, count, 0).astype(BF16), qg), slots)
    return dk, dv


def key_grad_body(
    off, place, dk0, dv0, dk1, dv1, mid_a, mid_b, far_a, far_b, own, grad_k, grad_v
):
    start = pl.multiple_of(place[0] * (PLANE * FAR_SLOT), PLANE * FAR_SLOT)
    far = jnp.concatenate([far_a[...], far_b[...]], axis=0)
    mid = jnp.concatenate([mid_a[...], mid_b[...]], axis=0)
    near_far = jnp.concatenate(
        [far_a[pl.ds(start, PLANE * FAR_SLOT), :], far_b[pl.ds(start, PLANE * FAR_SLOT), :]], axis=0
    ).astype(F32)
    lines2 = near_far.reshape(2 * PLANE, FAR_SLOT, WIDTH)
    lines3 = far.astype(F32).reshape(2 * CHIPS, FAR_SLOT, WIDTH)
    own32 = own[...].astype(F32)
    lse2 = stat_expand(lines2[:, 6, :], 2 * PLANE * 48, 48, -2 * MID, 3 * MID, 16)
    delta2 = stat_expand(lines2[:, 7, :], 2 * PLANE * 48, 48, -2 * MID, 3 * MID, 16)
    dk2, dv2 = far_key_grad(mid, own32[0:16], own32[16:32], lse2, delta2, 16, 48, MID, 2 * MID)
    lse3 = stat_expand(lines3[:, 6, :], 2 * CHIPS * FAR_SLOT, FAR_SLOT, MID, FAR, 8)
    delta3 = stat_expand(lines3[:, 7, :], 2 * CHIPS * FAR_SLOT, FAR_SLOT, MID, FAR, 8)
    dk3, dv3 = far_key_grad(far, own32[64:72], own32[80:88], lse3, delta3, 8, FAR_SLOT, FAR, 0)
    token = iota((TOK, WIDTH), 0)
    taken = [token % SPANS[b] == offset_row(off, b) for b in range(3)]
    for out, base, one, two, three in (
        (grad_k, dk0, dk1, dk2, dk3),
        (grad_v, dv0, dv1, dv2, dv3),
    ):
        total = base[...]
        for t, s in zip(
            taken,
            (
                spread_tok(one[...], NEAR, SPAN_NEAR),
                spread_tok(two, 16, SPAN_MID),
                spread_tok(three, 8, SPAN_ALL),
            ),
        ):
            total = total + jnp.where(t, s, 0.0)
        out[...] = total.astype(BF16)


def flip(value, mask):
    pairs = [(source, source ^ mask) for source in range(lax.axis_size("seq"))]
    return lax.ppermute(value, "seq", pairs)


def exchange(value, groups):
    return lax.all_to_all(value, "seq", 0, 0, tiled=True, axis_index_groups=groups)


def near_gather(value):
    core = flip(value, 1)
    other = flip(value, 2)
    return value, core, other, flip(other, 1)


def on_device(queries, keys, values, grad_out, offsets):
    devices = lax.axis_size("seq")
    chip_groups = [list(range(c, devices, 2)) for c in range(2)]
    plane_groups = [
        list(range(z * 2 * PLANE + c, (z + 1) * 2 * PLANE, 2))
        for z in range(devices // (2 * PLANE))
        for c in range(2)
    ]
    place = (lax.axis_index("seq") // (2 * PLANE)).astype(jnp.int32).reshape(1)

    near_kv, near_qg, mid_rep, far_rep, far_qg, own = call(
        select_body,
        [
            shape(2 * NEAR, WIDTH, BF16),
            shape(2 * NEAR, WIDTH, BF16),
            shape(PLANE * 48, WIDTH, BF16),
            shape(CHIPS * FAR_SLOT, WIDTH, BF16),
            shape(16, WIDTH, BF16),
            shape(128, WIDTH, BF16),
        ],
        [pltpu.VMEM((4 * PAIRS * TOK + 8, LANES), F32), pltpu.VMEM((64, WIDTH), F32)],
        5,
    )(offsets, queries, keys, values, grad_out)

    far_a = exchange(far_rep, chip_groups)
    mid_a = exchange(mid_rep, plane_groups)
    near_kvs = near_gather(near_kv)
    near_qgs = near_gather(near_qg)
    far_b = flip(far_a, 1)
    mid_b = flip(mid_a, 1)

    out0, peak0, total0 = call(
        local_forward_body,
        [shape(WIDTH, TOK, F32), shape(16, TOK, F32), shape(16, TOK, F32)],
        (),
        3,
        (),
    )(queries, keys, values)
    out1, peak1, total1 = call(
        near_forward_body,
        [shape(WIDTH, LANES, F32), shape(16, LANES, F32), shape(16, LANES, F32)],
        (),
        5,
        (),
    )(near_qg, *near_kvs)
    attended, lse, delta, near_stat, far_send = call(
        merge_body,
        [
            shape(TOK, WIDTH, BF16),
            shape(16, TOK, F32),
            shape(16, TOK, F32),
            shape(32, LANES, F32),
            shape(CHIPS * FAR_SLOT, WIDTH, BF16),
        ],
        (),
        14,
    )(
        offsets, grad_out, out0, peak0, total0, out1, peak1, total1,
        mid_a, mid_b, far_a, far_b, own, far_qg,
    )

    back_a = exchange(far_send, chip_groups)
    back_b = flip(back_a, 1)
    near_stats = near_gather(near_stat)

    dq_t, dk0, dv0 = call(
        local_backward_body,
        [shape(WIDTH, TOK, F32), shape(TOK, WIDTH, F32), shape(TOK, WIDTH, F32)],
        (),
        6,
        (),
    )(queries, keys, values, grad_out, lse, delta)
    grad_q = call(
        query_grad_body,
        shape(TOK, WIDTH, BF16),
        [pltpu.VMEM((WIDTH, LANES), F32)],
        15,
    )(
        offsets, near_qg, *near_kvs, mid_a, mid_b, far_a, far_b, own, lse, delta, near_stat, dq_t
    )
    dk1, dv1 = call(
        near_key_body,
        [shape(NEAR, WIDTH, F32), shape(NEAR, WIDTH, F32)],
        (),
        9,
        (),
    )(near_kv, *near_qgs, *near_stats)
    grad_k, grad_v = call(
        key_grad_body,
        [shape(TOK, WIDTH, BF16), shape(TOK, WIDTH, BF16)],
        (),
        11,
        (0, 1),
    )(offsets, place, dk0, dv0, dk1, dv1, mid_a, mid_b, back_a, back_b, own)
    return attended, grad_q, grad_k, grad_v


def solution(mesh):
    placed = (P("seq", None), P("seq", None), P("seq", None), P("seq", None), P())
    return jax.shard_map(
        on_device,
        mesh=mesh,
        in_specs=placed,
        out_specs=(P("seq", None),) * 4,
        check_vma=False,
    )
```

```python
import jax
import jax.numpy as jnp
from jax import lax
from jax.experimental import pallas as pl
from jax.experimental.pallas import tpu as pltpu
from jax.sharding import PartitionSpec as P

HEADS = 12
HEAD_DIM = 64
PAIRS = 6
LANES = 128
WIDTH = 768
TOK = 384
SPAN_NEAR = 4
SPAN_MID = 32
SPAN_ALL = 128
SPANS = (SPAN_NEAR, SPAN_MID, SPAN_ALL)
NEAR = TOK // SPAN_NEAR
MID = TOK // SPAN_MID
FAR = TOK // SPAN_ALL
MID_SLOT = 2 * MID
FAR_SLOT = 8
SHIFTS = (2, 5, 7)
CHUNKS = 2
CHIPS = 64
PLANE = 16
SCALE = 0.125
NEGATIVE = -1e30
F32 = jnp.float32
BF16 = jnp.bfloat16


def iota(shape, axis):
    return lax.broadcasted_iota(jnp.int32, shape, axis)


def nt(a, b):
    return lax.dot_general(a, b, (((1,), (1,)), ((), ())), preferred_element_type=F32)


def nn(a, b):
    return lax.dot_general(a, b, (((1,), (0,)), ((), ())), preferred_element_type=F32)


def tn(a, b):
    return lax.dot_general(a, b, (((0,), (0,)), ((), ())), preferred_element_type=F32)


def one_hot(test):
    return jnp.where(test, 1.0, 0.0).astype(BF16)


def thirds(x):
    first = x.astype(BF16)
    rest = x - first.astype(F32)
    second = rest.astype(BF16)
    return first, second, (rest - second.astype(F32)).astype(BF16)


def exact_nn(x, pick):
    rows = x.shape[0]
    y = nn(jnp.concatenate(thirds(x), axis=0), pick)
    return y[0:rows] + y[rows : 2 * rows] + y[2 * rows :]


def halves(x):
    hi = x.astype(BF16)
    return hi, (x - hi.astype(F32)).astype(BF16)


def offset_row(offsets_ref, branch):
    head = iota((1, WIDTH), 1) >> 6
    row = jnp.zeros((1, WIDTH), jnp.int32)
    for h in range(HEADS):
        row = jnp.where(head == h, offsets_ref[branch, h], row)
    return row


def offset_column(offsets_ref, branch):
    head = iota((16, 1), 0)
    column = jnp.zeros((16, 1), jnp.int32)
    for h in range(HEADS):
        column = jnp.where(head == h, offsets_ref[branch, h], column)
    return column


def head_taken(offsets_ref):
    token = iota((16, TOK), 1)
    return [(token & (SPANS[b] - 1)) == offset_column(offsets_ref, b) for b in range(3)]


def pair_block(x):
    lane = iota(x.shape, 1)
    zero = jnp.zeros((), x.dtype)
    return jnp.concatenate(
        [jnp.where(lane < HEAD_DIM, x, zero), jnp.where(lane >= HEAD_DIM, x, zero)], axis=0
    )


def head_lanes():
    return iota((HEADS, 1, WIDTH), 2) >> 6 == iota((HEADS, 1, WIDTH), 0)


def head_block(x, slots):
    return jnp.where(head_lanes(), x[None], 0.0).reshape(HEADS * slots, WIDTH).astype(BF16)


def head_sum(x, slots):
    return jnp.sum(jnp.where(head_lanes(), x.reshape(HEADS, slots, WIDTH), 0.0), axis=0)


def stat_up(rows, slots, shift):
    count = HEADS * slots
    bits = slots.bit_length() - 1
    own = iota((16, count), 1) >> bits == iota((16, count), 0)
    wide = jnp.concatenate([jnp.where(own, r, 0.0) for r in rows], axis=0)
    up = one_hot((iota((count, TOK), 0) & (slots - 1)) == iota((count, TOK), 1) >> shift)
    y = exact_nn(wide, up)
    return [y[16 * i : 16 * (i + 1)] for i in range(len(rows))]


def stat_down(xs, slots, shift):
    count = HEADS * slots
    bits = slots.bit_length() - 1
    down = one_hot(iota((TOK, count), 0) >> shift == (iota((TOK, count), 1) & (slots - 1)))
    wide = exact_nn(jnp.concatenate(xs, axis=0), down)
    keep = iota((16, count), 1) >> bits == iota((16, count), 0)
    return [
        jnp.sum(jnp.where(keep, wide[16 * i : 16 * (i + 1)], 0.0), axis=0, keepdims=True)
        for i in range(len(xs))
    ]


def spread_t(x, slots, shift):
    both = jnp.concatenate(halves(x), axis=0)
    up = one_hot(
        (iota((2 * slots, TOK), 0) & (slots - 1)) == iota((2 * slots, TOK), 1) >> shift
    )
    return tn(both, up)


def spread_tok(x, slots, shift):
    hi, lo = halves(x)
    up = one_hot(iota((TOK, slots), 1) == iota((TOK, slots), 0) >> shift)
    if slots < 64:
        return nn(jnp.concatenate([up, up], axis=1), jnp.concatenate([hi, lo], axis=0))
    return nn(up, hi) + nn(up, lo)


def spread_near_t(x):
    up = one_hot((iota((2 * LANES, TOK), 0) & (LANES - 1)) == iota((2 * LANES, TOK), 1) >> 2)
    return nn(jnp.concatenate(halves(x), axis=1), up)


def in_slots(rows, slot_rows, low, high, columns):
    slot = iota((rows // slot_rows, slot_rows, columns), 1)
    return ((slot >= low) & (slot < high)).reshape(rows, columns)


def call(
    body, out_shape, scratch=(), n_in=0, smem=(0,), cost=5, hbm=(), hbm_out=(), held=(), held_out=(),
    kept=(), kept_out=(),
):
    places = []
    for i in range(n_in):
        space = pltpu.SMEM if i in smem else pltpu.HBM if i in hbm else pltpu.VMEM
        places.append(pl.BlockSpec(memory_space=space))
    outs = [
        pl.BlockSpec(memory_space=pltpu.HBM if i in hbm_out else pltpu.VMEM)
        for i in range(len(out_shape))
    ]
    low_out = set(hbm_out) | set(held_out)
    shapes = []
    for i, x in enumerate(out_shape):
        space = pltpu.HBM if i in low_out else pltpu.VMEM if i in kept_out else None
        shapes.append(x if space is None else space(x.shape, x.dtype))
    kernel = pl.pallas_call(
        body,
        out_shape=shapes,
        in_specs=places,
        out_specs=outs,
        scratch_shapes=list(scratch),
        compiler_params=pltpu.CompilerParams(vmem_limit_bytes=16 * 1024 * 1024),
        cost_estimate=pl.CostEstimate(
            flops=cost * 1000000000, bytes_accessed=cost * 3000000, transcendentals=0
        ),
    )
    low = set(hbm) | set(held)

    def run(*operands):
        placed = []
        for i, x in enumerate(operands):
            space = pltpu.HBM if i in low else pltpu.VMEM if i in kept else None
            placed.append(x if space is None else pltpu.with_memory_space_constraint(x, space))
        return kernel(*placed)

    return run


def token_copies(sources, targets, sems):
    copies = []
    step = TOK // CHUNKS
    for a, (src, dst) in enumerate(zip(sources, targets)):
        for c in range(CHUNKS):
            rows = pl.ds(c * step, step)
            copies.append(
                pltpu.make_async_copy(src.at[rows, :], dst.at[rows, :], sems.at[a, c])
            )
            copies[-1].start()
    return copies


def wait(copies):
    for c in copies:
        c.wait()


def shape(rows, cols, dtype):
    return jax.ShapeDtypeStruct((rows, cols), dtype)


def select_body(
    off, q, k, v, g, near_kv, near_qg, mid_kvqg, far_kv, far_qg, own, vq, vk, vv,
    vg, wide, tmp, sems, near, far_tile, out_sems,
):
    staged = (vk, vv, vq, vg)
    copies = token_copies((k, v, q, g), staged, sems)
    first = iota((1, LANES), 1) < HEAD_DIM
    valid = iota((8, WIDTH), 0) < 2 * FAR
    tmp[...] = jnp.zeros((64, WIDTH), F32)
    outs = []
    for a in range(4):
        wait(copies[a * CHUNKS : (a + 1) * CHUNKS])
        for p in range(PAIRS):
            lanes = slice(p * LANES, (p + 1) * LANES)
            h = 2 * p
            base = (a * PAIRS + p) * TOK
            wide[base : base + TOK, :] = staged[a][:, lanes].astype(F32)
            a0 = wide[pl.ds(base + off[0, h], NEAR, stride=SPAN_NEAR), :]
            a1 = wide[pl.ds(base + off[0, h + 1], NEAR, stride=SPAN_NEAR), :]
            near[a * NEAR : (a + 1) * NEAR, lanes] = jnp.where(first, a0, a1).astype(BF16)
            for i in range(MID):
                b0 = wide[pl.ds(base + off[1, h] + i * SPAN_MID, 1), :]
                b1 = wide[pl.ds(base + off[1, h + 1] + i * SPAN_MID, 1), :]
                tmp[a * MID + i : a * MID + i + 1, lanes] = jnp.where(first, b0, b1)
            for i in range(FAR):
                c0 = wide[pl.ds(base + off[2, h] + i * SPAN_ALL, 1), :]
                c1 = wide[pl.ds(base + off[2, h + 1] + i * SPAN_ALL, 1), :]
                tmp[48 + a * FAR + i : 48 + a * FAR + i + 1, lanes] = jnp.where(first, c0, c1)
        if a == 1:
            kv8 = jnp.where(valid, tmp[48:56, :], 0.0)
            kv16 = jnp.concatenate([kv8, kv8], axis=0).astype(BF16)
            for d in range(CHIPS // 2):
                far_tile[d * 16 : (d + 1) * 16, :] = kv16
            outs.append(pltpu.make_async_copy(far_tile, far_kv, out_sems.at[2]))
            outs[-1].start()
        if a % 2 == 1:
            part = a // 2
            outs.append(
                pltpu.make_async_copy(
                    near.at[pl.ds(part * 2 * NEAR, 2 * NEAR), :],
                    (near_kv, near_qg)[part],
                    out_sems.at[part],
                )
            )
            outs[-1].start()
    mid_kvqg[...] = tmp[0:48, :].astype(BF16)
    far_qg[...] = jnp.concatenate([jnp.where(valid, tmp[54:62, :], 0.0)] * 2, axis=0).astype(BF16)
    row = iota((16, WIDTH), 0)
    for a in range(4):
        own[a * 16 : (a + 1) * 16, :] = jnp.where(
            row < MID, tmp[a * MID : a * MID + 16, :], 0.0
        ).astype(BF16)
        part = tmp[48 + a * FAR : 48 + a * FAR + 3, :]
        part = jnp.concatenate([part, jnp.zeros((13, WIDTH), F32)], axis=0)
        own[64 + a * 16 : 64 + (a + 1) * 16, :] = part.astype(BF16)
    wait(outs)


def local_forward_body(q, k, v, out_t, peak, total):
    peak[...] = jnp.zeros((16, TOK), F32)
    total[...] = jnp.ones((16, TOK), F32)
    for p in range(PAIRS):
        lanes = slice(p * LANES, (p + 1) * LANES)
        s = SCALE * nt(k[:, lanes], pair_block(q[:, lanes]))
        m = jnp.max(s, axis=0, keepdims=True)
        w = jnp.exp(s - m)
        t = jnp.sum(w, axis=0, keepdims=True)
        o = tn(v[:, lanes], w.astype(BF16))
        for e in range(2):
            cols = slice(e * TOK, (e + 1) * TOK)
            rows = slice(p * LANES + e * HEAD_DIM, p * LANES + (e + 1) * HEAD_DIM)
            out_t[rows, :] = o[e * HEAD_DIM : (e + 1) * HEAD_DIM, cols]
            peak[2 * p + e : 2 * p + e + 1, :] = m[:, cols]
            total[2 * p + e : 2 * p + e + 1, :] = t[:, cols]


def near_pair(refs, part, lanes):
    return jnp.concatenate([r[part * NEAR : (part + 1) * NEAR, lanes] for r in refs], axis=0)


def near_queries(ref, part, lanes):
    x = ref[part * NEAR : (part + 1) * NEAR, lanes]
    return pair_block(jnp.concatenate([x, jnp.zeros((LANES - NEAR, LANES), x.dtype)], axis=0))


def near_forward_body(qg, kv0, kv1, kv2, kv3, out_t, peak, total):
    refs = (kv0, kv1, kv2, kv3)
    peak[...] = jnp.zeros((16, LANES), F32)
    total[...] = jnp.ones((16, LANES), F32)
    for p in range(PAIRS):
        lanes = slice(p * LANES, (p + 1) * LANES)
        s = SCALE * nt(near_pair(refs, 0, lanes), near_queries(qg, 0, lanes))
        m = jnp.max(s, axis=0, keepdims=True)
        w = jnp.exp(s - m)
        t = jnp.sum(w, axis=0, keepdims=True)
        o = tn(near_pair(refs, 1, lanes), w.astype(BF16))
        for e in range(2):
            cols = slice(e * LANES, (e + 1) * LANES)
            rows = slice(p * LANES + e * HEAD_DIM, p * LANES + (e + 1) * HEAD_DIM)
            out_t[rows, :] = o[e * HEAD_DIM : (e + 1) * HEAD_DIM, cols]
            peak[2 * p + e : 2 * p + e + 1, :] = m[:, cols]
            total[2 * p + e : 2 * p + e + 1, :] = t[:, cols]


def far_forward(kv, query, slots, slot_rows, count):
    s = SCALE * nt(kv, head_block(query, slots))
    s = jnp.where(in_slots(s.shape[0], slot_rows, 0, count, s.shape[1]), s, NEGATIVE)
    m = jnp.max(s, axis=0, keepdims=True)
    w = jnp.exp(s - m)
    t = jnp.sum(w, axis=0, keepdims=True)
    o = tn(pltpu.roll(w, count, 0).astype(BF16), kv)
    return m, t, head_sum(o, slots)


def mid_forward_body(own, *rest):
    mids, (out2, peak2, total2) = rest[:8], rest[8:]
    m, t, o = far_forward(stack(mids), own[32:48, :].astype(F32), 16, MID_SLOT, MID)
    out2[...] = o
    peak2[...] = m
    total2[...] = t


def far_forward_body(far_a, far_b, own, out3, peak3, total3):
    far = jnp.concatenate([far_a[...], far_b[...]], axis=0)
    m, t, o = far_forward(far, own[96:112, :].astype(F32)[0:8], 8, FAR_SLOT, FAR)
    out3[...] = o
    peak3[...] = m
    total3[...] = t


def stack(refs):
    return jnp.concatenate([r[...] for r in refs], axis=0)


def merge_body(
    off, g, out0, peak0, total0, out1, peak1, total1, out2, peak2, total2,
    out3, peak3, total3, far_qg, attended, lse_ref, delta_ref, near_stat, far_send,
):
    taken = head_taken(off)
    up1 = one_hot(iota((LANES, TOK), 0) == iota((LANES, TOK), 1) >> 2)
    near = exact_nn(jnp.concatenate([peak1[...], total1[...]], axis=0), up1)
    mid = stat_up([peak2[...], total2[...]], 16, SHIFTS[1])
    far = stat_up([peak3[...], total3[...]], 8, SHIFTS[2])
    peaks = [near[0:16], mid[0], far[0]]
    totals = [near[16:32], mid[1], far[1]]
    peaks = [jnp.where(t, x, NEGATIVE) for t, x in zip(taken, peaks)]
    best = peak0[...]
    for x in peaks:
        best = jnp.maximum(best, x)
    den = total0[...] * jnp.exp(peak0[...] - best)
    for x, y, t in zip(peaks, totals, taken):
        den = den + jnp.where(t, y * jnp.exp(x - best), 0.0)
    lse = best + jnp.log(den)
    weight0 = jnp.exp(peak0[...] - lse)
    weights = [jnp.where(t, jnp.exp(x - lse), 0.0) for x, t in zip(peaks, taken)]
    s1 = spread_near_t(out1[...])
    s2 = spread_t(out2[...], 16, SHIFTS[1])
    s3 = spread_t(out3[...], 8, SHIFTS[2])
    parts = []
    for h in range(HEADS):
        rows = slice(h * HEAD_DIM, (h + 1) * HEAD_DIM)
        one = slice(h, h + 1)
        parts.append(
            out0[rows, :] * weight0[one]
            + s1[rows] * weights[0][one]
            + s2[rows] * weights[1][one]
            + s3[rows] * weights[2][one]
        )
    att = jnp.concatenate(parts, axis=0).T.astype(BF16)
    attended[...] = att
    hi, lo = halves(g[...].astype(F32) * att.astype(F32))
    pick = one_hot(iota((16, WIDTH), 1) >> 6 == iota((16, WIDTH), 0))
    delta = nt(pick, hi) + nt(pick, lo)
    lse_ref[...] = lse
    delta_ref[...] = delta
    down1 = one_hot(iota((TOK, LANES), 1) == iota((TOK, LANES), 0) >> 2)
    near_stat[...] = exact_nn(
        jnp.concatenate([jnp.where(taken[0], lse, 0.0), jnp.where(taken[0], delta, 0.0)], axis=0),
        down1,
    )
    column = iota((TOK, 256), 1) & 15
    row = iota((TOK, 256), 0)
    down2 = one_hot(row >> SHIFTS[1] == column)
    down3 = one_hot((row >> SHIFTS[2]) + MID == column)
    wide = exact_nn(
        jnp.concatenate([jnp.where(taken[1], lse, 0.0), jnp.where(taken[1], delta, 0.0)], axis=0),
        down2,
    ) + exact_nn(
        jnp.concatenate([jnp.where(taken[2], lse, 0.0), jnp.where(taken[2], delta, 0.0)], axis=0),
        down3,
    )
    keep = iota((16, 256), 1) >> 4 == iota((16, 256), 0)
    lines = []
    for e in range(2):
        line = jnp.sum(jnp.where(keep, wide[16 * e : 16 * e + 16], 0.0), axis=0, keepdims=True)
        lines.append(jnp.concatenate([x.astype(F32) for x in thirds(line)], axis=1))
    r = iota((16, WIDTH), 0) & 7
    send = jnp.where(r == 6, lines[0], jnp.where(r == 7, lines[1], far_qg[...].astype(F32)))
    send = send.astype(BF16)
    for d in range(CHIPS // 2):
        far_send[d * 16 : (d + 1) * 16, :] = send


def far_query_grad(kv, query, grad, lse, delta, slots, slot_rows, count):
    s = SCALE * nt(kv, head_block(query, slots))
    valid = in_slots(s.shape[0], slot_rows, 0, count, s.shape[1])
    prob = jnp.exp(jnp.where(valid, s - lse, NEGATIVE))
    dp = nt(kv, head_block(grad, slots))
    dp = pltpu.roll(dp, dp.shape[0] - count, 0)
    ds = jnp.where(valid, prob * (dp - delta), 0.0).astype(BF16)
    return SCALE * head_sum(tn(ds, kv), slots)


def local_grad_body(
    off, q_hbm, k_hbm, v_hbm, g_hbm, qg, kv0, kv1, kv2, kv3, far_a, far_b, own, lse, delta,
    near_stat, *rest
):
    mids, (grad_q, dk, dv, near_t, q, k, v, g, sems) = rest[:8], rest[8:]
    copies = token_copies((q_hbm, k_hbm, v_hbm, g_hbm), (q, k, v, g), sems)
    refs = (kv0, kv1, kv2, kv3)
    for p in range(PAIRS):
        lanes = slice(p * LANES, (p + 1) * LANES)
        h = 2 * p
        lr = jnp.concatenate([near_stat[h : h + 1, :], near_stat[h + 1 : h + 2, :]], axis=1)
        dr = jnp.concatenate([near_stat[16 + h : 17 + h, :], near_stat[17 + h : 18 + h, :]], axis=1)
        keys = near_pair(refs, 0, lanes)
        prob = jnp.exp(SCALE * nt(keys, near_queries(qg, 0, lanes)) - lr)
        dp = nt(near_pair(refs, 1, lanes), near_queries(qg, 1, lanes))
        ds = (prob * (dp - dr)).astype(BF16)
        dq = SCALE * tn(keys, ds)
        for e in range(2):
            rows = slice(p * LANES + e * HEAD_DIM, p * LANES + (e + 1) * HEAD_DIM)
            near_t[rows, :] = dq[e * HEAD_DIM : (e + 1) * HEAD_DIM, e * LANES : (e + 1) * LANES]
    taken = head_taken(off)
    far = jnp.concatenate([far_a[...], far_b[...]], axis=0)
    down = []
    for b, slots in ((1, 16), (2, 8)):
        down += stat_down([jnp.where(taken[b], x[...], 0.0) for x in (lse, delta)], slots, SHIFTS[b])
    dq2 = far_query_grad(
        stack(mids), own[32:48, :].astype(F32), own[48:64, :].astype(F32),
        down[0], down[1], 16, MID_SLOT, MID,
    )
    dq3 = far_query_grad(
        far, own[96:112, :].astype(F32)[0:8], own[112:128, :].astype(F32)[0:8],
        down[2], down[3], 8, FAR_SLOT, FAR,
    )
    s1 = spread_near_t(near_t[...])
    s2 = spread_t(dq2, 16, SHIFTS[1])
    s3 = spread_t(dq3, 8, SHIFTS[2])
    wait(copies)
    for p in range(PAIRS):
        lanes = slice(p * LANES, (p + 1) * LANES)
        qb = pair_block(q[:, lanes])
        gb = pair_block(g[:, lanes])
        lr = jnp.concatenate([lse[2 * p : 2 * p + 1, :], lse[2 * p + 1 : 2 * p + 2, :]], axis=1)
        dr = jnp.concatenate([delta[2 * p : 2 * p + 1, :], delta[2 * p + 1 : 2 * p + 2, :]], axis=1)
        prob = jnp.exp(SCALE * nt(k[:, lanes], qb) - lr)
        ds = (prob * (nt(v[:, lanes], gb) - dr)).astype(BF16)
        dv[p * TOK : (p + 1) * TOK, :] = nn(prob.astype(BF16), gb)
        dk[p * TOK : (p + 1) * TOK, :] = SCALE * nn(ds, qb)
        dq = SCALE * tn(k[:, lanes], ds)
        parts = []
        for e in range(2):
            h = 2 * p + e
            rows = slice(h * HEAD_DIM, (h + 1) * HEAD_DIM)
            total = dq[e * HEAD_DIM : (e + 1) * HEAD_DIM, e * TOK : (e + 1) * TOK]
            for t, x in zip(taken, (s1, s2, s3)):
                total = total + jnp.where(t[h : h + 1], x[rows], 0.0)
            parts.append(total)
        grad_q[:, lanes] = jnp.concatenate(parts, axis=0).T.astype(BF16)


def near_key_body(
    kv, qg0, qg1, qg2, qg3, st0, st1, st2, st3, dk_near, dv_near
):
    for p in range(PAIRS):
        lanes = slice(p * LANES, (p + 1) * LANES)
        kb = pair_block(kv[0:NEAR, lanes])
        vb = pair_block(kv[NEAR : 2 * NEAR, lanes])
        head = iota((2 * NEAR, NEAR), 0) < NEAR
        dk = jnp.zeros((2 * NEAR, LANES), F32)
        dv = jnp.zeros((2 * NEAR, LANES), F32)
        for qg, st in ((qg0, st0), (qg1, st1), (qg2, st2), (qg3, st3)):
            h = 2 * p
            queries = qg[0:NEAR, lanes]
            grads = qg[NEAR : 2 * NEAR, lanes]
            lr = jnp.where(head, st[h : h + 1, 0:NEAR], st[h + 1 : h + 2, 0:NEAR])
            dr = jnp.where(head, st[16 + h : 17 + h, 0:NEAR], st[17 + h : 18 + h, 0:NEAR])
            prob = jnp.exp(SCALE * nt(kb, queries) - lr)
            ds = (prob * (nt(vb, grads) - dr)).astype(BF16)
            dk = dk + nn(ds, queries)
            dv = dv + nn(prob.astype(BF16), grads)
        first = iota((NEAR, LANES), 1) < HEAD_DIM
        dk_near[:, lanes] = SCALE * jnp.where(first, dk[0:NEAR], dk[NEAR:])
        dv_near[:, lanes] = jnp.where(first, dv[0:NEAR], dv[NEAR:])


def stat_expand(line, slot_rows, first, low, count, slots):
    devices = line.shape[0]
    slot = iota((1, slot_rows, WIDTH), 1) - low
    mask = ((iota((1, slot_rows, WIDTH), 2) & 15) == slot + first) & (slot >= 0) & (slot < count)
    x = jnp.where(mask, line[:, None, :], 0.0).reshape(devices * slot_rows, WIDTH).astype(BF16)
    columns = HEADS * slots
    bits = slots.bit_length() - 1
    pick = one_hot(
        (iota((WIDTH, columns), 0) & 255) >> 4 == iota((WIDTH, columns), 1) >> bits
    )
    return nn(x, pick)


def far_key_grad(qg, key, value, lse, delta, slots, slot_rows, count):
    rows = qg.shape[0]
    s = SCALE * nt(qg, head_block(key, slots))
    valid = in_slots(rows, slot_rows, 0, count, s.shape[1])
    prob = jnp.exp(jnp.where(valid, s - lse, NEGATIVE))
    dp = nt(qg, head_block(value, slots))
    dp = pltpu.roll(dp, rows - count, 0)
    ds = jnp.where(valid, prob * (dp - delta), 0.0).astype(BF16)
    dk = SCALE * head_sum(tn(ds, qg), slots)
    dv = head_sum(tn(pltpu.roll(prob, count, 0).astype(BF16), qg), slots)
    return dk, dv


def key_grad_body(off, place, dk0, dv0, dk1, dv1, far_a, far_b, own, *rest):
    mids, (grad_k_hbm, grad_v_hbm, grad_k, grad_v, sems) = rest[:8], rest[8:]
    far = jnp.concatenate([far_a[...], far_b[...]], axis=0)
    own32 = own[...].astype(F32)
    line = iota((64, 2 * CHIPS * FAR_SLOT), 0)
    chip = (line & 15) ^ place[0]
    source = ((line >> 4) & 1) * (CHIPS * FAR_SLOT) + chip * FAR_SLOT + 6 + (line >> 5)
    lines2 = nn(one_hot(iota(line.shape, 1) == source), far)
    lines3 = far.astype(F32).reshape(2 * CHIPS, FAR_SLOT, WIDTH)
    lse2 = stat_expand(lines2[0:32], MID_SLOT, 0, 0, MID, 16)
    delta2 = stat_expand(lines2[32:64], MID_SLOT, 0, 0, MID, 16)
    dk2, dv2 = far_key_grad(stack(mids), own32[0:16], own32[16:32], lse2, delta2, 16, MID_SLOT, MID)
    lse3 = stat_expand(lines3[:, 6, :], FAR_SLOT, MID, 0, FAR, 8)
    delta3 = stat_expand(lines3[:, 7, :], FAR_SLOT, MID, 0, FAR, 8)
    dk3, dv3 = far_key_grad(far, own32[64:72], own32[80:88], lse3, delta3, 8, FAR_SLOT, FAR)
    token = iota((TOK, WIDTH), 0)
    taken = [(token & (SPANS[b] - 1)) == offset_row(off, b) for b in range(3)]
    outs = []
    for out, hbm, base, one, two, three in (
        (grad_k, grad_k_hbm, dk0, dk1, dk2, dk3),
        (grad_v, grad_v_hbm, dv0, dv1, dv2, dv3),
    ):
        total = jnp.concatenate([base[p * TOK : (p + 1) * TOK, :] for p in range(PAIRS)], axis=1)
        total = total + jnp.where(taken[0], spread_tok(one[...], NEAR, SHIFTS[0]), 0.0)
        total = total + jnp.where(taken[1], spread_tok(two, 16, SHIFTS[1]), 0.0)
        total = total + jnp.where(taken[2], spread_tok(three, 8, SHIFTS[2]), 0.0)
        out[...] = total.astype(BF16)
        outs.append(pltpu.make_async_copy(out, hbm, sems.at[len(outs)]))
        outs[-1].start()
    wait(outs)


def flip(value, mask):
    pairs = [(source, source ^ mask) for source in range(lax.axis_size("seq"))]
    return lax.ppermute(value, "seq", pairs)


def exchange(value, groups):
    return lax.all_to_all(value, "seq", 0, 0, tiled=True, axis_index_groups=groups)


def near_first(value):
    return value, flip(value, 1), flip(value, 2)


def near_direct(value):
    return value, flip(value, 1), flip(value, 2), flip(value, 3)


def near_second(values):
    return tuple(values) + (flip(values[2], 1),)


def near_gather(value):
    return near_second(near_first(value))


def plane_row(block):
    return [block] + [flip(block, d) for d in (8, 16, 24)]


def after(values, *deps):
    held = lax.optimization_barrier((tuple(values), tuple(deps)))
    return held[0]


def on_device(queries, keys, values, grad_out, offsets):
    devices = lax.axis_size("seq")
    chip_groups = [list(range(c, devices, 2)) for c in range(2)]
    place = (lax.axis_index("seq") >> 1).astype(jnp.int32).reshape(1)

    near_kv, near_qg, mid_kvqg, far_rep, far_qg, own, q_in, k_in, v_in = call(
        select_body,
        [
            shape(2 * NEAR, WIDTH, BF16),
            shape(2 * NEAR, WIDTH, BF16),
            shape(2 * MID_SLOT, WIDTH, BF16),
            shape(CHIPS * FAR_SLOT, WIDTH, BF16),
            shape(16, WIDTH, BF16),
            shape(128, WIDTH, BF16),
        ]
        + [shape(TOK, WIDTH, BF16)] * 3,
        [
            pltpu.VMEM((TOK, WIDTH), BF16),
            pltpu.VMEM((4 * PAIRS * TOK + 8, LANES), F32),
            pltpu.VMEM((64, WIDTH), F32),
            pltpu.SemaphoreType.DMA((4, CHUNKS)),
            pltpu.VMEM((4 * NEAR, WIDTH), BF16),
            pltpu.VMEM((CHIPS * FAR_SLOT, WIDTH), BF16),
            pltpu.SemaphoreType.DMA((3,)),
        ],
        5,
        hbm=(1, 2, 3, 4),
        hbm_out=(0, 1, 3),
        held=(0,),
        held_out=(2, 4, 5),
        kept_out=(6, 7, 8),
    )(offsets, queries, keys, values, grad_out)

    far_a = exchange(far_rep, chip_groups)
    lines = [mid_kvqg] + [flip(mid_kvqg, d) for d in (2, 4, 6)]
    near_kvs = near_gather(near_kv)
    mid_kv = jnp.concatenate([x[:MID_SLOT] for x in lines], axis=0)
    mid_qg = jnp.concatenate([x[MID_SLOT:] for x in lines], axis=0)
    mid_kvs = plane_row(mid_kv)

    out0, peak0, total0 = call(
        local_forward_body,
        [shape(WIDTH, TOK, F32), shape(16, TOK, F32), shape(16, TOK, F32)],
        (),
        3,
        (),
        kept=(0, 1, 2),
        kept_out=(0, 1, 2),
    )(q_in, after((k_in,), mid_kv)[0], v_in)
    out1, peak1, total1 = call(
        near_forward_body,
        [shape(WIDTH, LANES, F32), shape(16, LANES, F32), shape(16, LANES, F32)],
        (),
        5,
        (),
        1,
        held=(0, 1, 2, 3, 4),
        kept_out=(0, 1, 2),
    )(after((near_qg,), peak0)[0], *near_kvs)
    near_qgs = near_first(after((near_qg,), peak0)[0])
    mid_kvs = after(mid_kvs, peak1)
    far_a = after((far_a,), *mid_kvs)[0]
    far_b = flip(far_a, 1)
    near_qgs = near_second(after(near_qgs, far_a))
    mid_qgs = plane_row(after((mid_qg,), far_a)[0])
    mid_kvs = list(mid_kvs) + [flip(x, 1) for x in mid_kvs]
    out2, peak2, total2 = call(
        mid_forward_body,
        [shape(16, WIDTH, F32), shape(1, 192, F32), shape(1, 192, F32)],
        (),
        9,
        (),
        held=tuple(range(9)),
        kept_out=(0, 1, 2),
    )(own, *mid_kvs)
    out3, peak3, total3 = call(
        far_forward_body,
        [shape(8, WIDTH, F32), shape(1, 96, F32), shape(1, 96, F32)],
        (),
        3,
        (),
        held=(0, 1, 2),
        kept_out=(0, 1, 2),
    )(far_a, far_b, after((own,), peak2)[0])
    attended, lse, delta, near_stat, far_send = call(
        merge_body,
        [
            shape(TOK, WIDTH, BF16),
            shape(16, TOK, F32),
            shape(16, TOK, F32),
            shape(32, LANES, F32),
            shape(CHIPS * FAR_SLOT, WIDTH, BF16),
        ],
        (),
        15,
        held=(0, 1, 14),
        kept=tuple(range(2, 14)),
        held_out=(0, 3, 4),
        kept_out=(1, 2),
    )(
        offsets, grad_out, out0, peak0, total0, out1, peak1, total1, out2, peak2, total2,
        out3, peak3, total3, far_qg,
    )

    back_a = exchange(far_send, chip_groups)
    near_stats = near_direct(near_stat)
    mid_qgs = after(mid_qgs, lse)
    near_qg = after((near_qg,), lse, *mid_qgs, *near_qgs)[0]
    mid_qgs = list(mid_qgs) + [flip(x, 1) for x in mid_qgs]

    grad_q, dk0, dv0 = call(
        local_grad_body,
        [
            shape(TOK, WIDTH, BF16),
            shape(PAIRS * TOK, LANES, F32),
            shape(PAIRS * TOK, LANES, F32),
        ],
        [pltpu.VMEM((WIDTH, LANES), F32)]
        + [pltpu.VMEM((TOK, WIDTH), BF16)] * 4
        + [pltpu.SemaphoreType.DMA((4, CHUNKS))],
        24,
        cost=10,
        held=(0,) + tuple(range(5, 13)) + tuple(range(15, 24)),
        hbm=(1, 2, 3, 4),
        kept=(13, 14),
        held_out=(0,),
        kept_out=(1, 2),
    )(
        offsets, queries, keys, values, grad_out, near_qg, *near_kvs, far_a, far_b, own, lse,
        delta, near_stat, *mid_kvs,
    )
    back_a = after((back_a,), grad_q, *near_stats, *mid_qgs)[0]
    back_b = flip(back_a, 1)
    dk1, dv1 = call(
        near_key_body,
        [shape(NEAR, WIDTH, F32), shape(NEAR, WIDTH, F32)],
        (),
        9,
        (),
        held=tuple(range(9)),
        kept_out=(0, 1),
    )(after((near_kv,), back_a)[0], *near_qgs, *near_stats)
    grad_k, grad_v = call(
        key_grad_body,
        [shape(TOK, WIDTH, BF16), shape(TOK, WIDTH, BF16)],
        [
            pltpu.VMEM((TOK, WIDTH), BF16),
            pltpu.VMEM((TOK, WIDTH), BF16),
            pltpu.SemaphoreType.DMA((2,)),
        ],
        17,
        (0, 1),
        hbm_out=(0, 1),
        held=tuple(range(6, 17)),
        kept=(2, 3, 4, 5),
    )(offsets, place, dk0, dv0, dk1, dv1, back_a, back_b, own, *mid_qgs)
    return attended, grad_q, grad_k, grad_v


def solution(mesh):
    placed = (P("seq", None), P("seq", None), P("seq", None), P("seq", None), P())
    return jax.shard_map(
        on_device,
        mesh=mesh,
        in_specs=placed,
        out_specs=(P("seq", None),) * 4,
        check_vma=False,
    )
```

```python
import jax
import jax.numpy as jnp
from jax import lax
from jax.experimental import pallas as pl
from jax.experimental.pallas import tpu as pltpu
from jax.sharding import PartitionSpec as P

HEADS = 12
HEAD_DIM = 64
PAIRS = 6
LANES = 128
WIDTH = 768
TOK = 384
SPAN_NEAR = 4
SPAN_MID = 32
SPAN_ALL = 128
SPANS = (SPAN_NEAR, SPAN_MID, SPAN_ALL)
NEAR = TOK // SPAN_NEAR
MID = TOK // SPAN_MID
FAR = TOK // SPAN_ALL
MID_SLOT = 2 * MID
FAR_SLOT = 8
SHIFTS = (2, 5, 7)
CHUNKS = 2
CHIPS = 64
PLANE = 16
SCALE = 0.125
NEGATIVE = -1e30
F32 = jnp.float32
BF16 = jnp.bfloat16


def iota(shape, axis):
    return lax.broadcasted_iota(jnp.int32, shape, axis)


def nt(a, b):
    return lax.dot_general(a, b, (((1,), (1,)), ((), ())), preferred_element_type=F32)


def nn(a, b):
    return lax.dot_general(a, b, (((1,), (0,)), ((), ())), preferred_element_type=F32)


def tn(a, b):
    return lax.dot_general(a, b, (((0,), (0,)), ((), ())), preferred_element_type=F32)


def one_hot(test):
    return jnp.where(test, 1.0, 0.0).astype(BF16)


def thirds(x):
    first = x.astype(BF16)
    rest = x - first.astype(F32)
    second = rest.astype(BF16)
    return first, second, (rest - second.astype(F32)).astype(BF16)


def exact_nn(x, pick):
    rows = x.shape[0]
    y = nn(jnp.concatenate(thirds(x), axis=0), pick)
    return y[0:rows] + y[rows : 2 * rows] + y[2 * rows :]


def halves(x):
    hi = x.astype(BF16)
    return hi, (x - hi.astype(F32)).astype(BF16)


def offset_row(offsets_ref, branch):
    head = iota((1, WIDTH), 1) >> 6
    row = jnp.zeros((1, WIDTH), jnp.int32)
    for h in range(HEADS):
        row = jnp.where(head == h, offsets_ref[branch, h], row)
    return row


def offset_column(offsets_ref, branch):
    head = iota((16, 1), 0)
    column = jnp.zeros((16, 1), jnp.int32)
    for h in range(HEADS):
        column = jnp.where(head == h, offsets_ref[branch, h], column)
    return column


def head_taken(offsets_ref):
    token = iota((16, TOK), 1)
    return [(token & (SPANS[b] - 1)) == offset_column(offsets_ref, b) for b in range(3)]


def pair_block(x):
    lane = iota(x.shape, 1)
    zero = jnp.zeros((), x.dtype)
    return jnp.concatenate(
        [jnp.where(lane < HEAD_DIM, x, zero), jnp.where(lane >= HEAD_DIM, x, zero)], axis=0
    )


def heads_of(slots):
    return 16 if slots == 8 else HEADS


def head_lanes(heads):
    return iota((heads, 1, WIDTH), 2) >> 6 == iota((heads, 1, WIDTH), 0)


def head_block(x, slots):
    heads = heads_of(slots)
    return jnp.where(head_lanes(heads), x[None], 0.0).reshape(heads * slots, WIDTH).astype(BF16)


def head_sum(x, slots):
    heads = heads_of(slots)
    return jnp.sum(jnp.where(head_lanes(heads), x.reshape(heads, slots, WIDTH), 0.0), axis=0)


def stat_up(rows, slots, shift):
    count = heads_of(slots) * slots
    bits = slots.bit_length() - 1
    own = iota((16, count), 1) >> bits == iota((16, count), 0)
    wide = jnp.concatenate([jnp.where(own, r, 0.0) for r in rows], axis=0)
    up = one_hot((iota((count, TOK), 0) & (slots - 1)) == iota((count, TOK), 1) >> shift)
    y = exact_nn(wide, up)
    return [y[16 * i : 16 * (i + 1)] for i in range(len(rows))]


def stat_down(xs, slots, shift):
    count = heads_of(slots) * slots
    bits = slots.bit_length() - 1
    down = one_hot(iota((TOK, count), 0) >> shift == (iota((TOK, count), 1) & (slots - 1)))
    wide = exact_nn(jnp.concatenate(xs, axis=0), down)
    keep = iota((16, count), 1) >> bits == iota((16, count), 0)
    return [
        jnp.sum(jnp.where(keep, wide[16 * i : 16 * (i + 1)], 0.0), axis=0, keepdims=True)
        for i in range(len(xs))
    ]


def spread_t(x, slots, shift):
    both = jnp.concatenate(halves(x), axis=0)
    up = one_hot(
        (iota((2 * slots, TOK), 0) & (slots - 1)) == iota((2 * slots, TOK), 1) >> shift
    )
    return tn(both, up)


def spread_tok(x, slots, shift):
    hi, lo = halves(x)
    up = one_hot(iota((TOK, slots), 1) == iota((TOK, slots), 0) >> shift)
    if slots < 64:
        return nn(jnp.concatenate([up, up], axis=1), jnp.concatenate([hi, lo], axis=0))
    return nn(up, hi) + nn(up, lo)


def spread_near_t(x):
    up = one_hot((iota((2 * LANES, TOK), 0) & (LANES - 1)) == iota((2 * LANES, TOK), 1) >> 2)
    return nn(jnp.concatenate(halves(x), axis=1), up)


def in_slots(rows, slot_rows, low, high, columns):
    slot = iota((rows // slot_rows, slot_rows, columns), 1)
    return ((slot >= low) & (slot < high)).reshape(rows, columns)


def call(
    body, out_shape, scratch=(), n_in=0, smem=(0,), cost=5, hbm=(), hbm_out=(), held=(), held_out=(),
    kept=(), kept_out=(),
):
    places = []
    for i in range(n_in):
        space = pltpu.SMEM if i in smem else pltpu.HBM if i in hbm else pltpu.VMEM
        places.append(pl.BlockSpec(memory_space=space))
    outs = [
        pl.BlockSpec(memory_space=pltpu.HBM if i in hbm_out else pltpu.VMEM)
        for i in range(len(out_shape))
    ]
    low_out = set(hbm_out) | set(held_out)
    shapes = []
    for i, x in enumerate(out_shape):
        space = pltpu.HBM if i in low_out else pltpu.VMEM if i in kept_out else None
        shapes.append(x if space is None else space(x.shape, x.dtype))
    kernel = pl.pallas_call(
        body,
        out_shape=shapes,
        in_specs=places,
        out_specs=outs,
        scratch_shapes=list(scratch),
        compiler_params=pltpu.CompilerParams(vmem_limit_bytes=16 * 1024 * 1024),
        cost_estimate=pl.CostEstimate(
            flops=cost * 1000000000, bytes_accessed=cost * 3000000, transcendentals=0
        ),
    )
    low = set(hbm) | set(held)

    def run(*operands):
        placed = []
        for i, x in enumerate(operands):
            space = pltpu.HBM if i in low else pltpu.VMEM if i in kept else None
            placed.append(x if space is None else pltpu.with_memory_space_constraint(x, space))
        return kernel(*placed)

    return run


def token_copies(sources, targets, sems):
    copies = []
    step = TOK // CHUNKS
    for a, (src, dst) in enumerate(zip(sources, targets)):
        for c in range(CHUNKS):
            rows = pl.ds(c * step, step)
            copies.append(
                pltpu.make_async_copy(src.at[rows, :], dst.at[rows, :], sems.at[a, c])
            )
            copies[-1].start()
    return copies


def wait(copies):
    for c in copies:
        c.wait()


def shape(rows, cols, dtype):
    return jax.ShapeDtypeStruct((rows, cols), dtype)


def select_body(
    off, q, k, v, g, near_kv, near_qg, mid_kvqg, far_kv, far_qg, own, vq, vk, vv,
    vg, wide, tmp, sems, near, far_tile, out_sems,
):
    staged = (vk, vv, vq, vg)
    copies = token_copies((k, v, q, g), staged, sems)
    first = iota((1, LANES), 1) < HEAD_DIM
    valid = iota((8, WIDTH), 0) < 2 * FAR
    tmp[...] = jnp.zeros((64, WIDTH), F32)
    outs = []
    for a in range(4):
        wait(copies[a * CHUNKS : (a + 1) * CHUNKS])
        for p in range(PAIRS):
            lanes = slice(p * LANES, (p + 1) * LANES)
            h = 2 * p
            base = (a * PAIRS + p) * TOK
            wide[base : base + TOK, :] = staged[a][:, lanes].astype(F32)
            a0 = wide[pl.ds(base + off[0, h], NEAR, stride=SPAN_NEAR), :]
            a1 = wide[pl.ds(base + off[0, h + 1], NEAR, stride=SPAN_NEAR), :]
            near[a * NEAR : (a + 1) * NEAR, lanes] = jnp.where(first, a0, a1).astype(BF16)
            for i in range(MID):
                b0 = wide[pl.ds(base + off[1, h] + i * SPAN_MID, 1), :]
                b1 = wide[pl.ds(base + off[1, h + 1] + i * SPAN_MID, 1), :]
                tmp[a * MID + i : a * MID + i + 1, lanes] = jnp.where(first, b0, b1)
            for i in range(FAR):
                c0 = wide[pl.ds(base + off[2, h] + i * SPAN_ALL, 1), :]
                c1 = wide[pl.ds(base + off[2, h + 1] + i * SPAN_ALL, 1), :]
                tmp[48 + a * FAR + i : 48 + a * FAR + i + 1, lanes] = jnp.where(first, c0, c1)
        if a == 1:
            kv8 = jnp.where(valid, tmp[48:56, :], 0.0)
            kv16 = jnp.concatenate([kv8, kv8], axis=0).astype(BF16)
            for d in range(CHIPS // 2):
                far_tile[d * 16 : (d + 1) * 16, :] = kv16
            outs.append(pltpu.make_async_copy(far_tile, far_kv, out_sems.at[2]))
            outs[-1].start()
        if a % 2 == 1:
            part = a // 2
            outs.append(
                pltpu.make_async_copy(
                    near.at[pl.ds(part * 2 * NEAR, 2 * NEAR), :],
                    (near_kv, near_qg)[part],
                    out_sems.at[part],
                )
            )
            outs[-1].start()
    mid_kvqg[...] = tmp[0:48, :].astype(BF16)
    far_qg[...] = jnp.concatenate([jnp.where(valid, tmp[54:62, :], 0.0)] * 2, axis=0).astype(BF16)
    row = iota((16, WIDTH), 0)
    for a in range(4):
        own[a * 16 : (a + 1) * 16, :] = jnp.where(
            row < MID, tmp[a * MID : a * MID + 16, :], 0.0
        ).astype(BF16)
        part = tmp[48 + a * FAR : 48 + a * FAR + 3, :]
        part = jnp.concatenate([part, jnp.zeros((13, WIDTH), F32)], axis=0)
        own[64 + a * 16 : 64 + (a + 1) * 16, :] = part.astype(BF16)
    wait(outs)


def local_forward_body(q, k, v, out_t, peak, total):
    peak[...] = jnp.zeros((16, TOK), F32)
    total[...] = jnp.ones((16, TOK), F32)
    for p in range(PAIRS):
        lanes = slice(p * LANES, (p + 1) * LANES)
        s = SCALE * nt(k[:, lanes], pair_block(q[:, lanes]))
        m = jnp.max(s, axis=0, keepdims=True)
        w = jnp.exp(s - m)
        t = jnp.sum(w, axis=0, keepdims=True)
        o = tn(v[:, lanes], w.astype(BF16))
        for e in range(2):
            cols = slice(e * TOK, (e + 1) * TOK)
            rows = slice(p * LANES + e * HEAD_DIM, p * LANES + (e + 1) * HEAD_DIM)
            out_t[rows, :] = o[e * HEAD_DIM : (e + 1) * HEAD_DIM, cols]
            peak[2 * p + e : 2 * p + e + 1, :] = m[:, cols]
            total[2 * p + e : 2 * p + e + 1, :] = t[:, cols]


def near_pair(refs, part, lanes):
    return jnp.concatenate([r[part * NEAR : (part + 1) * NEAR, lanes] for r in refs], axis=0)


def near_queries(ref, part, lanes):
    x = ref[part * NEAR : (part + 1) * NEAR, lanes]
    return pair_block(jnp.concatenate([x, jnp.zeros((LANES - NEAR, LANES), x.dtype)], axis=0))


def near_forward_body(qg, kv0, kv1, kv2, kv3, out_t, peak, total):
    refs = (kv0, kv1, kv2, kv3)
    peak[...] = jnp.zeros((16, LANES), F32)
    total[...] = jnp.ones((16, LANES), F32)
    for p in range(PAIRS):
        lanes = slice(p * LANES, (p + 1) * LANES)
        s = SCALE * nt(near_pair(refs, 0, lanes), near_queries(qg, 0, lanes))
        m = jnp.max(s, axis=0, keepdims=True)
        w = jnp.exp(s - m)
        t = jnp.sum(w, axis=0, keepdims=True)
        o = tn(near_pair(refs, 1, lanes), w.astype(BF16))
        for e in range(2):
            cols = slice(e * LANES, (e + 1) * LANES)
            rows = slice(p * LANES + e * HEAD_DIM, p * LANES + (e + 1) * HEAD_DIM)
            out_t[rows, :] = o[e * HEAD_DIM : (e + 1) * HEAD_DIM, cols]
            peak[2 * p + e : 2 * p + e + 1, :] = m[:, cols]
            total[2 * p + e : 2 * p + e + 1, :] = t[:, cols]


def softmax_parts(s):
    m = jnp.max(s, axis=0, keepdims=True)
    w = jnp.exp(s - m)
    return m, w, jnp.sum(w, axis=0, keepdims=True)


def stack(refs, part):
    return jnp.concatenate([r[part * 48 : part * 48 + 48, :] for r in refs], axis=0)


def mid_forward_body(own, *rest):
    mids, (out2, peak2, total2) = rest[:8], rest[8:]
    s = SCALE * nt(stack(mids, 0), head_block(own[32:48, :].astype(F32), 16))
    peak2[...], w, total2[...] = softmax_parts(s)
    out2[...] = head_sum(tn(w.astype(BF16), stack(mids, 1)), 16)


def far_forward_body(far_a, far_b, own, out3, peak3, total3):
    far = jnp.concatenate([far_a[...], far_b[...]], axis=0)
    s = SCALE * nt(far, head_block(own[96:112, :].astype(F32)[0:8], 8))
    s = jnp.where(in_slots(s.shape[0], FAR_SLOT, 0, FAR, s.shape[1]), s, NEGATIVE)
    peak3[...], w, total3[...] = softmax_parts(s)
    out3[...] = head_sum(tn(pltpu.roll(w, FAR, 0).astype(BF16), far), 8)


def merge_body(
    off, g, out0, peak0, total0, out1, peak1, total1, out2, peak2, total2,
    out3, peak3, total3, far_qg, attended, lse_ref, delta_ref, near_stat, far_send,
):
    taken = head_taken(off)
    up1 = one_hot(iota((LANES, TOK), 0) == iota((LANES, TOK), 1) >> 2)
    near = exact_nn(jnp.concatenate([peak1[...], total1[...]], axis=0), up1)
    mid = stat_up([peak2[...], total2[...]], 16, SHIFTS[1])
    far = stat_up([peak3[...], total3[...]], 8, SHIFTS[2])
    peaks = [near[0:16], mid[0], far[0]]
    totals = [near[16:32], mid[1], far[1]]
    peaks = [jnp.where(t, x, NEGATIVE) for t, x in zip(taken, peaks)]
    best = peak0[...]
    for x in peaks:
        best = jnp.maximum(best, x)
    den = total0[...] * jnp.exp(peak0[...] - best)
    for x, y, t in zip(peaks, totals, taken):
        den = den + jnp.where(t, y * jnp.exp(x - best), 0.0)
    lse = best + jnp.log(den)
    weight0 = jnp.exp(peak0[...] - lse)
    weights = [jnp.where(t, jnp.exp(x - lse), 0.0) for x, t in zip(peaks, taken)]
    s1 = spread_near_t(out1[...])
    s2 = spread_t(out2[...], 16, SHIFTS[1])
    s3 = spread_t(out3[...], 8, SHIFTS[2])
    parts = []
    for h in range(HEADS):
        rows = slice(h * HEAD_DIM, (h + 1) * HEAD_DIM)
        one = slice(h, h + 1)
        parts.append(
            out0[rows, :] * weight0[one]
            + s1[rows] * weights[0][one]
            + s2[rows] * weights[1][one]
            + s3[rows] * weights[2][one]
        )
    att = jnp.concatenate(parts, axis=0).T.astype(BF16)
    attended[...] = att
    hi, lo = halves(g[...].astype(F32) * att.astype(F32))
    pick = one_hot(iota((16, WIDTH), 1) >> 6 == iota((16, WIDTH), 0))
    delta = nt(pick, hi) + nt(pick, lo)
    lse_ref[...] = lse
    delta_ref[...] = delta
    down1 = one_hot(iota((TOK, LANES), 1) == iota((TOK, LANES), 0) >> 2)
    near_stat[...] = exact_nn(
        jnp.concatenate([jnp.where(taken[0], lse, 0.0), jnp.where(taken[0], delta, 0.0)], axis=0),
        down1,
    )
    column = iota((TOK, 256), 1) & 15
    row = iota((TOK, 256), 0)
    down2 = one_hot(row >> SHIFTS[1] == column)
    down3 = one_hot((row >> SHIFTS[2]) + MID == column)
    wide = exact_nn(
        jnp.concatenate([jnp.where(taken[1], lse, 0.0), jnp.where(taken[1], delta, 0.0)], axis=0),
        down2,
    ) + exact_nn(
        jnp.concatenate([jnp.where(taken[2], lse, 0.0), jnp.where(taken[2], delta, 0.0)], axis=0),
        down3,
    )
    keep = iota((16, 256), 1) >> 4 == iota((16, 256), 0)
    lines = []
    for e in range(2):
        line = jnp.sum(jnp.where(keep, wide[16 * e : 16 * e + 16], 0.0), axis=0, keepdims=True)
        lines.append(jnp.concatenate([x.astype(F32) for x in thirds(line)], axis=1))
    r = iota((16, WIDTH), 0) & 7
    send = jnp.where(r == 6, lines[0], jnp.where(r == 7, lines[1], far_qg[...].astype(F32)))
    send = send.astype(BF16)
    for d in range(CHIPS // 2):
        far_send[d * 16 : (d + 1) * 16, :] = send


def far_products(rows, first, second):
    both = nt(rows, jnp.concatenate([head_block(first, 8), head_block(second, 8)], axis=0))
    return SCALE * both[:, 0:128], pltpu.roll(both[:, 128:256], rows.shape[0] - FAR, 0)


def far_query_grad(kv, query, grad, lse, delta):
    s, dp = far_products(kv, query, grad)
    valid = in_slots(s.shape[0], FAR_SLOT, 0, FAR, s.shape[1])
    prob = jnp.exp(jnp.where(valid, s - lse, NEGATIVE))
    ds = jnp.where(valid, prob * (dp - delta), 0.0).astype(BF16)
    return SCALE * head_sum(tn(ds, kv), 8)


def mid_query_grad(keys, values, query, grad, lse, delta):
    prob = jnp.exp(SCALE * nt(keys, head_block(query, 16)) - lse)
    ds = (prob * (nt(values, head_block(grad, 16)) - delta)).astype(BF16)
    return SCALE * head_sum(tn(ds, keys), 16)


def local_grad_body(
    off, q_hbm, k_hbm, v_hbm, g_hbm, qg, kv0, kv1, kv2, kv3, far_a, far_b, own, lse, delta,
    near_stat, *rest
):
    mids, (grad_q, dk, dv, near_t, q, k, v, g, sems) = rest[:8], rest[8:]
    copies = token_copies((q_hbm, k_hbm, v_hbm, g_hbm), (q, k, v, g), sems)
    refs = (kv0, kv1, kv2, kv3)
    for p in range(PAIRS):
        lanes = slice(p * LANES, (p + 1) * LANES)
        h = 2 * p
        lr = jnp.concatenate([near_stat[h : h + 1, :], near_stat[h + 1 : h + 2, :]], axis=1)
        dr = jnp.concatenate([near_stat[16 + h : 17 + h, :], near_stat[17 + h : 18 + h, :]], axis=1)
        keys = near_pair(refs, 0, lanes)
        prob = jnp.exp(SCALE * nt(keys, near_queries(qg, 0, lanes)) - lr)
        dp = nt(near_pair(refs, 1, lanes), near_queries(qg, 1, lanes))
        ds = (prob * (dp - dr)).astype(BF16)
        dq = SCALE * tn(keys, ds)
        for e in range(2):
            rows = slice(p * LANES + e * HEAD_DIM, p * LANES + (e + 1) * HEAD_DIM)
            near_t[rows, :] = dq[e * HEAD_DIM : (e + 1) * HEAD_DIM, e * LANES : (e + 1) * LANES]
    taken = head_taken(off)
    far = jnp.concatenate([far_a[...], far_b[...]], axis=0)
    down = []
    for b, slots in ((1, 16), (2, 8)):
        down += stat_down([jnp.where(taken[b], x[...], 0.0) for x in (lse, delta)], slots, SHIFTS[b])
    dq2 = mid_query_grad(
        stack(mids, 0), stack(mids, 1), own[32:48, :].astype(F32), own[48:64, :].astype(F32),
        down[0], down[1],
    )
    dq3 = far_query_grad(
        far, own[96:112, :].astype(F32)[0:8], own[112:128, :].astype(F32)[0:8], down[2], down[3]
    )
    s1 = spread_near_t(near_t[...])
    s2 = spread_t(dq2, 16, SHIFTS[1])
    s3 = spread_t(dq3, 8, SHIFTS[2])
    wait(copies)
    for p in range(PAIRS):
        lanes = slice(p * LANES, (p + 1) * LANES)
        qb = pair_block(q[:, lanes])
        gb = pair_block(g[:, lanes])
        lr = jnp.concatenate([lse[2 * p : 2 * p + 1, :], lse[2 * p + 1 : 2 * p + 2, :]], axis=1)
        dr = jnp.concatenate([delta[2 * p : 2 * p + 1, :], delta[2 * p + 1 : 2 * p + 2, :]], axis=1)
        prob = jnp.exp(SCALE * nt(k[:, lanes], qb) - lr)
        ds = (prob * (nt(v[:, lanes], gb) - dr)).astype(BF16)
        dv[p * TOK : (p + 1) * TOK, :] = nn(prob.astype(BF16), gb)
        dk[p * TOK : (p + 1) * TOK, :] = SCALE * nn(ds, qb)
        dq = SCALE * tn(k[:, lanes], ds)
        parts = []
        for e in range(2):
            h = 2 * p + e
            rows = slice(h * HEAD_DIM, (h + 1) * HEAD_DIM)
            total = dq[e * HEAD_DIM : (e + 1) * HEAD_DIM, e * TOK : (e + 1) * TOK]
            for t, x in zip(taken, (s1, s2, s3)):
                total = total + jnp.where(t[h : h + 1], x[rows], 0.0)
            parts.append(total)
        grad_q[:, lanes] = jnp.concatenate(parts, axis=0).T.astype(BF16)


def near_key_body(kv, qg0, qg1, qg2, qg3, st0, st1, st2, st3, dk_near, dv_near):
    refs = (qg0, qg1, qg2, qg3)
    stats = jnp.concatenate([st[:, 0:NEAR] for st in (st0, st1, st2, st3)], axis=1)
    head = iota((2 * NEAR, TOK), 0) < NEAR
    first = iota((NEAR, LANES), 1) < HEAD_DIM
    for p in range(PAIRS):
        lanes = slice(p * LANES, (p + 1) * LANES)
        h = 2 * p
        queries = near_pair(refs, 0, lanes)
        grads = near_pair(refs, 1, lanes)
        lr = jnp.where(head, stats[h : h + 1], stats[h + 1 : h + 2])
        dr = jnp.where(head, stats[16 + h : 17 + h], stats[17 + h : 18 + h])
        prob = jnp.exp(SCALE * nt(pair_block(kv[0:NEAR, lanes]), queries) - lr)
        ds = (prob * (nt(pair_block(kv[NEAR : 2 * NEAR, lanes]), grads) - dr)).astype(BF16)
        dk = nn(ds, queries)
        dv = nn(prob.astype(BF16), grads)
        dk_near[:, lanes] = SCALE * jnp.where(first, dk[0:NEAR], dk[NEAR:])
        dv_near[:, lanes] = jnp.where(first, dv[0:NEAR], dv[NEAR:])


def stat_pick(slots):
    columns = heads_of(slots) * slots
    bits = slots.bit_length() - 1
    return one_hot(
        (iota((WIDTH, columns), 0) & 255) >> 4 == iota((WIDTH, columns), 1) >> bits
    )


def far_expand(line, pick):
    slot = iota((1, FAR_SLOT, WIDTH), 1)
    mask = ((iota((1, FAR_SLOT, WIDTH), 2) & 15) == slot + MID) & (slot < FAR)
    x = jnp.where(mask, line[:, None, :], 0.0).reshape(line.shape[0] * FAR_SLOT, WIDTH)
    return nn(x.astype(BF16), pick)


def far_key_grad(qg, key, value, lse, delta):
    s, dp = far_products(qg, key, value)
    valid = in_slots(s.shape[0], FAR_SLOT, 0, FAR, s.shape[1])
    prob = jnp.exp(jnp.where(valid, s - lse, NEGATIVE))
    ds = jnp.where(valid, prob * (dp - delta), 0.0).astype(BF16)
    dk = SCALE * head_sum(tn(ds, qg), 8)
    dv = head_sum(tn(pltpu.roll(prob, FAR, 0).astype(BF16), qg), 8)
    return dk, dv


def mid_key_grad(queries, grads, key, value, lse, delta):
    prob = jnp.exp(SCALE * nt(queries, head_block(key, 16)) - lse)
    ds = (prob * (nt(grads, head_block(value, 16)) - delta)).astype(BF16)
    return SCALE * head_sum(tn(ds, queries), 16), head_sum(tn(prob.astype(BF16), grads), 16)


def key_grad_body(off, place, dk0, dv0, dk1, dv1, far_a, far_b, own, *rest):
    mids, (grad_k_hbm, grad_v_hbm, grad_k, grad_v, sems) = rest[:8], rest[8:]
    far = jnp.concatenate([far_a[...], far_b[...]], axis=0)
    own32 = own[...].astype(F32)
    line = iota((64, 2 * CHIPS * FAR_SLOT), 0)
    chip = (line & 15) ^ place[0]
    source = ((line >> 4) & 1) * (CHIPS * FAR_SLOT) + chip * FAR_SLOT + 6 + (line >> 5)
    lines2 = nn(one_hot(iota(line.shape, 1) == source), far)
    lines3 = far.astype(F32).reshape(2 * CHIPS, FAR_SLOT, WIDTH)
    device = iota((TOK, 32), 1) * MID
    row = iota((TOK, 32), 0)
    spread = one_hot((row >= device) & (row < device + MID))
    slot = lax.rem(iota((TOK, 1), 0), MID)
    mask = (iota((TOK, WIDTH), 1) & 15) == slot
    lines2 = lines2.astype(BF16)
    pick2 = stat_pick(16)
    lse2, delta2 = (
        nn(jnp.where(mask, nn(spread, lines2[32 * e : 32 * e + 32]), 0.0).astype(BF16), pick2)
        for e in range(2)
    )
    dk2, dv2 = mid_key_grad(stack(mids, 0), stack(mids, 1), own32[0:16], own32[16:32], lse2, delta2)
    pick3 = stat_pick(8)
    lse3 = far_expand(lines3[:, 6, :], pick3)
    delta3 = far_expand(lines3[:, 7, :], pick3)
    dk3, dv3 = far_key_grad(far, own32[64:72], own32[80:88], lse3, delta3)
    token = iota((TOK, WIDTH), 0)
    taken = [(token & (SPANS[b] - 1)) == offset_row(off, b) for b in range(3)]
    outs = []
    for out, hbm, base, one, two, three in (
        (grad_k, grad_k_hbm, dk0, dk1, dk2, dk3),
        (grad_v, grad_v_hbm, dv0, dv1, dv2, dv3),
    ):
        total = jnp.concatenate([base[p * TOK : (p + 1) * TOK, :] for p in range(PAIRS)], axis=1)
        total = total + jnp.where(taken[0], spread_tok(one[...], NEAR, SHIFTS[0]), 0.0)
        total = total + jnp.where(taken[1], spread_tok(two, 16, SHIFTS[1]), 0.0)
        total = total + jnp.where(taken[2], spread_tok(three, 8, SHIFTS[2]), 0.0)
        out[...] = total.astype(BF16)
        outs.append(pltpu.make_async_copy(out, hbm, sems.at[len(outs)]))
        outs[-1].start()
    wait(outs)


def flip(value, mask):
    pairs = [(source, source ^ mask) for source in range(lax.axis_size("seq"))]
    return lax.ppermute(value, "seq", pairs)


def exchange(value, groups):
    return lax.all_to_all(value, "seq", 0, 0, tiled=True, axis_index_groups=groups)


def near_first(value):
    return value, flip(value, 1), flip(value, 2)


def near_direct(value):
    return value, flip(value, 1), flip(value, 2), flip(value, 3)


def near_second(values):
    return tuple(values) + (flip(values[2], 1),)


def near_gather(value):
    return near_second(near_first(value))


def plane_row(block):
    return [block] + [flip(block, d) for d in (8, 16, 24)]


def after(values, *deps):
    held = lax.optimization_barrier((tuple(values), tuple(deps)))
    return held[0]


def on_device(queries, keys, values, grad_out, offsets):
    devices = lax.axis_size("seq")
    chip_groups = [list(range(c, devices, 2)) for c in range(2)]
    place = (lax.axis_index("seq") >> 1).astype(jnp.int32).reshape(1)

    near_kv, near_qg, mid_kvqg, far_rep, far_qg, own, q_in, k_in, v_in = call(
        select_body,
        [
            shape(2 * NEAR, WIDTH, BF16),
            shape(2 * NEAR, WIDTH, BF16),
            shape(2 * MID_SLOT, WIDTH, BF16),
            shape(CHIPS * FAR_SLOT, WIDTH, BF16),
            shape(16, WIDTH, BF16),
            shape(128, WIDTH, BF16),
        ]
        + [shape(TOK, WIDTH, BF16)] * 3,
        [
            pltpu.VMEM((TOK, WIDTH), BF16),
            pltpu.VMEM((4 * PAIRS * TOK + 8, LANES), F32),
            pltpu.VMEM((64, WIDTH), F32),
            pltpu.SemaphoreType.DMA((4, CHUNKS)),
            pltpu.VMEM((4 * NEAR, WIDTH), BF16),
            pltpu.VMEM((CHIPS * FAR_SLOT, WIDTH), BF16),
            pltpu.SemaphoreType.DMA((3,)),
        ],
        5,
        hbm=(1, 2, 3, 4),
        hbm_out=(0, 1, 3),
        held=(0,),
        held_out=(2, 4, 5),
        kept_out=(6, 7, 8),
    )(offsets, queries, keys, values, grad_out)

    far_a = exchange(far_rep, chip_groups)
    lines = [mid_kvqg] + [flip(mid_kvqg, d) for d in (2, 4, 6)]
    near_kvs = near_gather(near_kv)
    parts = [
        jnp.concatenate([x[a * MID : (a + 1) * MID] for x in lines], axis=0) for a in range(4)
    ]
    mid_kv = jnp.concatenate(parts[0:2], axis=0)
    mid_qg = jnp.concatenate(parts[2:4], axis=0)
    mid_kvs = plane_row(mid_kv)

    out0, peak0, total0 = call(
        local_forward_body,
        [shape(WIDTH, TOK, F32), shape(16, TOK, F32), shape(16, TOK, F32)],
        (),
        3,
        (),
        kept=(0, 1, 2),
        kept_out=(0, 1, 2),
    )(q_in, after((k_in,), mid_kv)[0], v_in)
    out1, peak1, total1 = call(
        near_forward_body,
        [shape(WIDTH, LANES, F32), shape(16, LANES, F32), shape(16, LANES, F32)],
        (),
        5,
        (),
        1,
        held=(0, 1, 2, 3, 4),
        kept_out=(0, 1, 2),
    )(after((near_qg,), peak0)[0], *near_kvs)
    near_qgs = near_first(after((near_qg,), mid_kv)[0])
    mid_kvs, near_qgs = after((tuple(mid_kvs), near_qgs), peak1)
    far_a = after((far_a,), *mid_kvs)[0]
    far_b = flip(far_a, 1)
    near_qgs = near_second(near_qgs)
    mid_kvs = list(mid_kvs) + [flip(x, 1) for x in mid_kvs]
    out2, peak2, total2 = call(
        mid_forward_body,
        [shape(16, WIDTH, F32), shape(1, 192, F32), shape(1, 192, F32)],
        (),
        9,
        (),
        held=tuple(range(9)),
        kept_out=(0, 1, 2),
    )(own, *mid_kvs)
    out3, peak3, total3 = call(
        far_forward_body,
        [shape(8, WIDTH, F32), shape(1, 128, F32), shape(1, 128, F32)],
        (),
        3,
        (),
        held=(0, 1, 2),
        kept_out=(0, 1, 2),
    )(far_a, far_b, after((own,), peak2)[0])
    attended, lse, delta, near_stat, far_send = call(
        merge_body,
        [
            shape(TOK, WIDTH, BF16),
            shape(16, TOK, F32),
            shape(16, TOK, F32),
            shape(32, LANES, F32),
            shape(CHIPS * FAR_SLOT, WIDTH, BF16),
        ],
        (),
        15,
        held=(0, 1, 14),
        kept=tuple(range(2, 14)),
        held_out=(0, 3, 4),
        kept_out=(1, 2),
    )(
        offsets, grad_out, out0, peak0, total0, out1, peak1, total1, out2, peak2, total2,
        out3, peak3, total3, far_qg,
    )

    back_a = exchange(far_send, chip_groups)
    near_stats = near_direct(near_stat)
    mid_qgs = plane_row(after((mid_qg,), lse)[0])
    near_qg = after((near_qg,), lse, *near_qgs)[0]

    grad_q, dk0, dv0 = call(
        local_grad_body,
        [
            shape(TOK, WIDTH, BF16),
            shape(PAIRS * TOK, LANES, F32),
            shape(PAIRS * TOK, LANES, F32),
        ],
        [pltpu.VMEM((WIDTH, LANES), F32)]
        + [pltpu.VMEM((TOK, WIDTH), BF16)] * 4
        + [pltpu.SemaphoreType.DMA((4, CHUNKS))],
        24,
        cost=10,
        held=(0,) + tuple(range(5, 13)) + tuple(range(15, 24)),
        hbm=(1, 2, 3, 4),
        kept=(13, 14),
        held_out=(0,),
        kept_out=(1, 2),
    )(
        offsets, queries, keys, values, grad_out, near_qg, *near_kvs, far_a, far_b, own, lse,
        delta, near_stat, *mid_kvs,
    )
    mid_qgs = after(mid_qgs, grad_q)
    back_a = after((back_a,), *mid_qgs, *near_stats)[0]
    mid_qgs = list(mid_qgs) + [flip(x, 1) for x in mid_qgs]
    back_b = flip(back_a, 1)
    dk1, dv1 = call(
        near_key_body,
        [shape(NEAR, WIDTH, F32), shape(NEAR, WIDTH, F32)],
        (),
        9,
        (),
        held=tuple(range(9)),
        kept_out=(0, 1),
    )(after((near_kv,), back_a)[0], *near_qgs, *near_stats)
    grad_k, grad_v = call(
        key_grad_body,
        [shape(TOK, WIDTH, BF16), shape(TOK, WIDTH, BF16)],
        [
            pltpu.VMEM((TOK, WIDTH), BF16),
            pltpu.VMEM((TOK, WIDTH), BF16),
            pltpu.SemaphoreType.DMA((2,)),
        ],
        17,
        (0, 1),
        hbm_out=(0, 1),
        held=tuple(range(6, 17)),
        kept=(2, 3, 4, 5),
    )(offsets, place, dk0, dv0, dk1, dv1, back_a, back_b, own, *mid_qgs)
    return attended, grad_q, grad_k, grad_v


def solution(mesh):
    placed = (P("seq", None), P("seq", None), P("seq", None), P("seq", None), P())
    return jax.shard_map(
        on_device,
        mesh=mesh,
        in_specs=placed,
        out_specs=(P("seq", None),) * 4,
        check_vma=False,
    )
```

```python
import jax
import jax.numpy as jnp
from jax import lax
from jax.experimental import pallas as pl
from jax.experimental.pallas import tpu as pltpu
from jax.sharding import PartitionSpec as P

HEADS = 12
HEAD_DIM = 64
PAIRS = 6
LANES = 128
WIDTH = 768
TOK = 384
SPAN_NEAR = 4
SPAN_MID = 32
SPAN_ALL = 128
SPANS = (SPAN_NEAR, SPAN_MID, SPAN_ALL)
NEAR = TOK // SPAN_NEAR
MID = TOK // SPAN_MID
FAR = TOK // SPAN_ALL
MID_SLOT = 2 * MID
FAR_SLOT = 8
SHIFTS = (2, 5, 7)
CHUNKS = 2
CHIPS = 64
PLANE = 16
SCALE = 0.125
NEGATIVE = -1e30
F32 = jnp.float32
BF16 = jnp.bfloat16


def iota(shape, axis):
    return lax.broadcasted_iota(jnp.int32, shape, axis)


def nt(a, b):
    return lax.dot_general(a, b, (((1,), (1,)), ((), ())), preferred_element_type=F32)


def nn(a, b):
    return lax.dot_general(a, b, (((1,), (0,)), ((), ())), preferred_element_type=F32)


def tn(a, b):
    return lax.dot_general(a, b, (((0,), (0,)), ((), ())), preferred_element_type=F32)


def one_hot(test):
    return jnp.where(test, 1.0, 0.0).astype(BF16)


def thirds(x):
    first = x.astype(BF16)
    rest = x - first.astype(F32)
    second = rest.astype(BF16)
    return first, second, (rest - second.astype(F32)).astype(BF16)


def exact_nn(x, pick):
    rows = x.shape[0]
    y = nn(jnp.concatenate(thirds(x), axis=0), pick)
    return y[0:rows] + y[rows : 2 * rows] + y[2 * rows :]


def halves(x):
    hi = x.astype(BF16)
    return hi, (x - hi.astype(F32)).astype(BF16)


def offset_row(offsets_ref, branch):
    head = iota((1, WIDTH), 1) >> 6
    row = jnp.zeros((1, WIDTH), jnp.int32)
    for h in range(HEADS):
        row = jnp.where(head == h, offsets_ref[branch, h], row)
    return row


def offset_column(offsets_ref, branch):
    head = iota((16, 1), 0)
    column = jnp.zeros((16, 1), jnp.int32)
    for h in range(HEADS):
        column = jnp.where(head == h, offsets_ref[branch, h], column)
    return column


def head_taken(offsets_ref):
    token = iota((16, TOK), 1)
    return [(token & (SPANS[b] - 1)) == offset_column(offsets_ref, b) for b in range(3)]


def pair_block(x):
    lane = iota(x.shape, 1)
    zero = jnp.zeros((), x.dtype)
    return jnp.concatenate(
        [jnp.where(lane < HEAD_DIM, x, zero), jnp.where(lane >= HEAD_DIM, x, zero)], axis=0
    )


def heads_of(slots):
    return 16 if slots == 8 else HEADS


def head_lanes(heads):
    return iota((heads, 1, WIDTH), 2) >> 6 == iota((heads, 1, WIDTH), 0)


def head_block(x, slots):
    heads = heads_of(slots)
    return jnp.where(head_lanes(heads), x[None], 0.0).reshape(heads * slots, WIDTH).astype(BF16)


def head_sum(x, slots):
    heads = heads_of(slots)
    return jnp.sum(jnp.where(head_lanes(heads), x.reshape(heads, slots, WIDTH), 0.0), axis=0)


def stat_up(rows, slots, shift):
    count = heads_of(slots) * slots
    bits = slots.bit_length() - 1
    own = iota((16, count), 1) >> bits == iota((16, count), 0)
    wide = jnp.concatenate([jnp.where(own, r, 0.0) for r in rows], axis=0)
    up = one_hot((iota((count, TOK), 0) & (slots - 1)) == iota((count, TOK), 1) >> shift)
    y = exact_nn(wide, up)
    return [y[16 * i : 16 * (i + 1)] for i in range(len(rows))]


def stat_down(xs, slots, shift):
    count = heads_of(slots) * slots
    bits = slots.bit_length() - 1
    down = one_hot(iota((TOK, count), 0) >> shift == (iota((TOK, count), 1) & (slots - 1)))
    wide = exact_nn(jnp.concatenate(xs, axis=0), down)
    keep = iota((16, count), 1) >> bits == iota((16, count), 0)
    return [
        jnp.sum(jnp.where(keep, wide[16 * i : 16 * (i + 1)], 0.0), axis=0, keepdims=True)
        for i in range(len(xs))
    ]


def spread_t(x, slots, shift):
    both = jnp.concatenate(halves(x), axis=0)
    up = one_hot(
        (iota((2 * slots, TOK), 0) & (slots - 1)) == iota((2 * slots, TOK), 1) >> shift
    )
    return tn(both, up)


def spread_tok(x, slots, shift):
    hi, lo = halves(x)
    up = one_hot(iota((TOK, slots), 1) == iota((TOK, slots), 0) >> shift)
    if slots < 64:
        return nn(jnp.concatenate([up, up], axis=1), jnp.concatenate([hi, lo], axis=0))
    return nn(up, hi) + nn(up, lo)


def spread_near_t(x):
    up = one_hot((iota((2 * LANES, TOK), 0) & (LANES - 1)) == iota((2 * LANES, TOK), 1) >> 2)
    return nn(jnp.concatenate(halves(x), axis=1), up)


def in_slots(rows, slot_rows, low, high, columns):
    slot = iota((rows // slot_rows, slot_rows, columns), 1)
    return ((slot >= low) & (slot < high)).reshape(rows, columns)


def call(
    body, out_shape, scratch=(), n_in=0, smem=(0,), cost=5, hbm=(), hbm_out=(), held=(), held_out=(),
    kept=(), kept_out=(),
):
    places = []
    for i in range(n_in):
        space = pltpu.SMEM if i in smem else pltpu.HBM if i in hbm else pltpu.VMEM
        places.append(pl.BlockSpec(memory_space=space))
    outs = [
        pl.BlockSpec(memory_space=pltpu.HBM if i in hbm_out else pltpu.VMEM)
        for i in range(len(out_shape))
    ]
    low_out = set(hbm_out) | set(held_out)
    shapes = []
    for i, x in enumerate(out_shape):
        space = pltpu.HBM if i in low_out else pltpu.VMEM if i in kept_out else None
        shapes.append(x if space is None else space(x.shape, x.dtype))
    kernel = pl.pallas_call(
        body,
        out_shape=shapes,
        in_specs=places,
        out_specs=outs,
        scratch_shapes=list(scratch),
        compiler_params=pltpu.CompilerParams(vmem_limit_bytes=16 * 1024 * 1024),
        cost_estimate=pl.CostEstimate(
            flops=cost * 1000000000, bytes_accessed=cost * 3000000, transcendentals=0
        ),
    )
    low = set(hbm) | set(held)

    def run(*operands):
        placed = []
        for i, x in enumerate(operands):
            space = pltpu.HBM if i in low else pltpu.VMEM if i in kept else None
            placed.append(x if space is None else pltpu.with_memory_space_constraint(x, space))
        return kernel(*placed)

    return run


def token_copies(sources, targets, sems):
    copies = []
    step = TOK // CHUNKS
    for a, (src, dst) in enumerate(zip(sources, targets)):
        for c in range(CHUNKS):
            rows = pl.ds(c * step, step)
            copies.append(
                pltpu.make_async_copy(src.at[rows, :], dst.at[rows, :], sems.at[a, c])
            )
            copies[-1].start()
    return copies


def wait(copies):
    for c in copies:
        c.wait()


def shape(rows, cols, dtype):
    return jax.ShapeDtypeStruct((rows, cols), dtype)


def select_body(
    off, q, k, v, g, near_kv, near_qg, mid_kvqg, far_kv, far_qg, own, vq, vk, vv,
    vg, wide, tmp, sems, near, far_tile, out_sems,
):
    staged = (vk, vv, vq, vg)
    copies = token_copies((k, v, q, g), staged, sems)
    first = iota((1, LANES), 1) < HEAD_DIM
    valid = iota((8, WIDTH), 0) < 2 * FAR
    tmp[...] = jnp.zeros((64, WIDTH), F32)
    outs = []
    for a in range(4):
        wait(copies[a * CHUNKS : (a + 1) * CHUNKS])
        for p in range(PAIRS):
            lanes = slice(p * LANES, (p + 1) * LANES)
            h = 2 * p
            base = (a * PAIRS + p) * TOK
            wide[base : base + TOK, :] = staged[a][:, lanes].astype(F32)
            a0 = wide[pl.ds(base + off[0, h], NEAR, stride=SPAN_NEAR), :]
            a1 = wide[pl.ds(base + off[0, h + 1], NEAR, stride=SPAN_NEAR), :]
            near[a * NEAR : (a + 1) * NEAR, lanes] = jnp.where(first, a0, a1).astype(BF16)
            for i in range(MID):
                b0 = wide[pl.ds(base + off[1, h] + i * SPAN_MID, 1), :]
                b1 = wide[pl.ds(base + off[1, h + 1] + i * SPAN_MID, 1), :]
                tmp[a * MID + i : a * MID + i + 1, lanes] = jnp.where(first, b0, b1)
            for i in range(FAR):
                c0 = wide[pl.ds(base + off[2, h] + i * SPAN_ALL, 1), :]
                c1 = wide[pl.ds(base + off[2, h + 1] + i * SPAN_ALL, 1), :]
                tmp[48 + a * FAR + i : 48 + a * FAR + i + 1, lanes] = jnp.where(first, c0, c1)
        if a == 1:
            kv8 = jnp.where(valid, tmp[48:56, :], 0.0)
            kv16 = jnp.concatenate([kv8, kv8], axis=0).astype(BF16)
            for d in range(CHIPS // 2):
                far_tile[d * 16 : (d + 1) * 16, :] = kv16
            outs.append(pltpu.make_async_copy(far_tile, far_kv, out_sems.at[2]))
            outs[-1].start()
        if a % 2 == 1:
            part = a // 2
            outs.append(
                pltpu.make_async_copy(
                    near.at[pl.ds(part * 2 * NEAR, 2 * NEAR), :],
                    (near_kv, near_qg)[part],
                    out_sems.at[part],
                )
            )
            outs[-1].start()
    mid_kvqg[...] = tmp[0:48, :].astype(BF16)
    far_qg[...] = jnp.concatenate([jnp.where(valid, tmp[54:62, :], 0.0)] * 2, axis=0).astype(BF16)
    row = iota((16, WIDTH), 0)
    for a in range(4):
        own[a * 16 : (a + 1) * 16, :] = jnp.where(
            row < MID, tmp[a * MID : a * MID + 16, :], 0.0
        ).astype(BF16)
        part = tmp[48 + a * FAR : 48 + a * FAR + 3, :]
        part = jnp.concatenate([part, jnp.zeros((13, WIDTH), F32)], axis=0)
        own[64 + a * 16 : 64 + (a + 1) * 16, :] = part.astype(BF16)
    wait(outs)


def local_forward_body(q, k, v, out_t, peak, total):
    peak[...] = jnp.zeros((16, TOK), F32)
    total[...] = jnp.ones((16, TOK), F32)
    for p in range(PAIRS):
        lanes = slice(p * LANES, (p + 1) * LANES)
        s = SCALE * nt(k[:, lanes], pair_block(q[:, lanes]))
        m = jnp.max(s, axis=0, keepdims=True)
        w = jnp.exp(s - m)
        t = jnp.sum(w, axis=0, keepdims=True)
        o = tn(v[:, lanes], w.astype(BF16))
        for e in range(2):
            cols = slice(e * TOK, (e + 1) * TOK)
            rows = slice(p * LANES + e * HEAD_DIM, p * LANES + (e + 1) * HEAD_DIM)
            out_t[rows, :] = o[e * HEAD_DIM : (e + 1) * HEAD_DIM, cols]
            peak[2 * p + e : 2 * p + e + 1, :] = m[:, cols]
            total[2 * p + e : 2 * p + e + 1, :] = t[:, cols]


def near_pair(refs, part, lanes):
    return jnp.concatenate([r[part * NEAR : (part + 1) * NEAR, lanes] for r in refs], axis=0)


def near_queries(ref, part, lanes):
    x = ref[part * NEAR : (part + 1) * NEAR, lanes]
    return pair_block(jnp.concatenate([x, jnp.zeros((LANES - NEAR, LANES), x.dtype)], axis=0))


def near_forward_body(qg, kv0, kv1, kv2, kv3, out_t, peak, total):
    refs = (kv0, kv1, kv2, kv3)
    peak[...] = jnp.zeros((16, LANES), F32)
    total[...] = jnp.ones((16, LANES), F32)
    for p in range(PAIRS):
        lanes = slice(p * LANES, (p + 1) * LANES)
        s = SCALE * nt(near_pair(refs, 0, lanes), near_queries(qg, 0, lanes))
        m = jnp.max(s, axis=0, keepdims=True)
        w = jnp.exp(s - m)
        t = jnp.sum(w, axis=0, keepdims=True)
        o = tn(near_pair(refs, 1, lanes), w.astype(BF16))
        for e in range(2):
            cols = slice(e * LANES, (e + 1) * LANES)
            rows = slice(p * LANES + e * HEAD_DIM, p * LANES + (e + 1) * HEAD_DIM)
            out_t[rows, :] = o[e * HEAD_DIM : (e + 1) * HEAD_DIM, cols]
            peak[2 * p + e : 2 * p + e + 1, :] = m[:, cols]
            total[2 * p + e : 2 * p + e + 1, :] = t[:, cols]


def softmax_parts(s):
    m = jnp.max(s, axis=0, keepdims=True)
    w = jnp.exp(s - m)
    return m, w, jnp.sum(w, axis=0, keepdims=True)


def stack(refs, part):
    return jnp.concatenate([r[part * 48 : part * 48 + 48, :] for r in refs], axis=0)


def mid_forward_body(own, *rest):
    mids, (out2, peak2, total2) = rest[:8], rest[8:]
    s = SCALE * nt(stack(mids, 0), head_block(own[32:48, :].astype(F32), 16))
    peak2[...], w, total2[...] = softmax_parts(s)
    out2[...] = head_sum(tn(w.astype(BF16), stack(mids, 1)), 16)


def far_forward_body(far_a, far_b, own, out3, peak3, total3):
    far = jnp.concatenate([far_a[...], far_b[...]], axis=0)
    s = SCALE * nt(far, head_block(own[96:112, :].astype(F32)[0:8], 8))
    s = jnp.where(in_slots(s.shape[0], FAR_SLOT, 0, FAR, s.shape[1]), s, NEGATIVE)
    peak3[...], w, total3[...] = softmax_parts(s)
    out3[...] = head_sum(tn(pltpu.roll(w, FAR, 0).astype(BF16), far), 8)


def merge_body(
    off, g, out0, peak0, total0, out1, peak1, total1, out2, peak2, total2,
    out3, peak3, total3, far_qg, attended, lse_ref, delta_ref, near_stat, far_send,
):
    taken = head_taken(off)
    up1 = one_hot(iota((LANES, TOK), 0) == iota((LANES, TOK), 1) >> 2)
    near = exact_nn(jnp.concatenate([peak1[...], total1[...]], axis=0), up1)
    mid = stat_up([peak2[...], total2[...]], 16, SHIFTS[1])
    far = stat_up([peak3[...], total3[...]], 8, SHIFTS[2])
    peaks = [near[0:16], mid[0], far[0]]
    totals = [near[16:32], mid[1], far[1]]
    peaks = [jnp.where(t, x, NEGATIVE) for t, x in zip(taken, peaks)]
    best = peak0[...]
    for x in peaks:
        best = jnp.maximum(best, x)
    den = total0[...] * jnp.exp(peak0[...] - best)
    for x, y, t in zip(peaks, totals, taken):
        den = den + jnp.where(t, y * jnp.exp(x - best), 0.0)
    lse = best + jnp.log(den)
    weight0 = jnp.exp(peak0[...] - lse)
    weights = [jnp.where(t, jnp.exp(x - lse), 0.0) for x, t in zip(peaks, taken)]
    s1 = spread_near_t(out1[...])
    s2 = spread_t(out2[...], 16, SHIFTS[1])
    s3 = spread_t(out3[...], 8, SHIFTS[2])
    parts = []
    for h in range(HEADS):
        rows = slice(h * HEAD_DIM, (h + 1) * HEAD_DIM)
        one = slice(h, h + 1)
        parts.append(
            out0[rows, :] * weight0[one]
            + s1[rows] * weights[0][one]
            + s2[rows] * weights[1][one]
            + s3[rows] * weights[2][one]
        )
    att = jnp.concatenate(parts, axis=0).T.astype(BF16)
    attended[...] = att
    hi, lo = halves(g[...].astype(F32) * att.astype(F32))
    pick = one_hot(iota((16, WIDTH), 1) >> 6 == iota((16, WIDTH), 0))
    delta = nt(pick, hi) + nt(pick, lo)
    lse_ref[...] = lse
    delta_ref[...] = delta
    down1 = one_hot(iota((TOK, LANES), 1) == iota((TOK, LANES), 0) >> 2)
    near_stat[...] = exact_nn(
        jnp.concatenate([jnp.where(taken[0], lse, 0.0), jnp.where(taken[0], delta, 0.0)], axis=0),
        down1,
    )
    column = iota((TOK, 256), 1) & 15
    row = iota((TOK, 256), 0)
    down2 = one_hot(row >> SHIFTS[1] == column)
    down3 = one_hot((row >> SHIFTS[2]) + MID == column)
    wide = exact_nn(
        jnp.concatenate([jnp.where(taken[1], lse, 0.0), jnp.where(taken[1], delta, 0.0)], axis=0),
        down2,
    ) + exact_nn(
        jnp.concatenate([jnp.where(taken[2], lse, 0.0), jnp.where(taken[2], delta, 0.0)], axis=0),
        down3,
    )
    keep = iota((16, 256), 1) >> 4 == iota((16, 256), 0)
    lines = []
    for e in range(2):
        line = jnp.sum(jnp.where(keep, wide[16 * e : 16 * e + 16], 0.0), axis=0, keepdims=True)
        lines.append(jnp.concatenate([x.astype(F32) for x in thirds(line)], axis=1))
    r = iota((16, WIDTH), 0) & 7
    send = jnp.where(r == 6, lines[0], jnp.where(r == 7, lines[1], far_qg[...].astype(F32)))
    send = send.astype(BF16)
    for d in range(CHIPS // 2):
        far_send[d * 16 : (d + 1) * 16, :] = send


def far_products(rows, first, second):
    both = nt(rows, jnp.concatenate([head_block(first, 8), head_block(second, 8)], axis=0))
    return SCALE * both[:, 0:128], pltpu.roll(both[:, 128:256], rows.shape[0] - FAR, 0)


def far_query_grad(kv, query, grad, lse, delta):
    s, dp = far_products(kv, query, grad)
    valid = in_slots(s.shape[0], FAR_SLOT, 0, FAR, s.shape[1])
    prob = jnp.exp(jnp.where(valid, s - lse, NEGATIVE))
    ds = jnp.where(valid, prob * (dp - delta), 0.0).astype(BF16)
    return SCALE * head_sum(tn(ds, kv), 8)


def mid_query_grad(keys, values, query, grad, lse, delta):
    prob = jnp.exp(SCALE * nt(keys, head_block(query, 16)) - lse)
    ds = (prob * (nt(values, head_block(grad, 16)) - delta)).astype(BF16)
    return SCALE * head_sum(tn(ds, keys), 16)


def local_grad_body(
    off, q_hbm, k_hbm, v_hbm, g_hbm, qg, kv0, kv1, kv2, kv3, far_a, far_b, own, lse, delta,
    near_stat, *rest
):
    mids, (grad_q, dk, dv, near_t, q, k, v, g, sems) = rest[:8], rest[8:]
    copies = token_copies((q_hbm, k_hbm, v_hbm, g_hbm), (q, k, v, g), sems)
    refs = (kv0, kv1, kv2, kv3)
    for p in range(PAIRS):
        lanes = slice(p * LANES, (p + 1) * LANES)
        h = 2 * p
        lr = jnp.concatenate([near_stat[h : h + 1, :], near_stat[h + 1 : h + 2, :]], axis=1)
        dr = jnp.concatenate([near_stat[16 + h : 17 + h, :], near_stat[17 + h : 18 + h, :]], axis=1)
        keys = near_pair(refs, 0, lanes)
        prob = jnp.exp(SCALE * nt(keys, near_queries(qg, 0, lanes)) - lr)
        dp = nt(near_pair(refs, 1, lanes), near_queries(qg, 1, lanes))
        ds = (prob * (dp - dr)).astype(BF16)
        dq = SCALE * tn(keys, ds)
        for e in range(2):
            rows = slice(p * LANES + e * HEAD_DIM, p * LANES + (e + 1) * HEAD_DIM)
            near_t[rows, :] = dq[e * HEAD_DIM : (e + 1) * HEAD_DIM, e * LANES : (e + 1) * LANES]
    taken = head_taken(off)
    far = jnp.concatenate([far_a[...], far_b[...]], axis=0)
    down = []
    for b, slots in ((1, 16), (2, 8)):
        down += stat_down([jnp.where(taken[b], x[...], 0.0) for x in (lse, delta)], slots, SHIFTS[b])
    dq2 = mid_query_grad(
        stack(mids, 0), stack(mids, 1), own[32:48, :].astype(F32), own[48:64, :].astype(F32),
        down[0], down[1],
    )
    dq3 = far_query_grad(
        far, own[96:112, :].astype(F32)[0:8], own[112:128, :].astype(F32)[0:8], down[2], down[3]
    )
    s1 = spread_near_t(near_t[...])
    s2 = spread_t(dq2, 16, SHIFTS[1])
    s3 = spread_t(dq3, 8, SHIFTS[2])
    wait(copies)
    for p in range(PAIRS):
        lanes = slice(p * LANES, (p + 1) * LANES)
        qb = pair_block(q[:, lanes])
        gb = pair_block(g[:, lanes])
        lr = jnp.concatenate([lse[2 * p : 2 * p + 1, :], lse[2 * p + 1 : 2 * p + 2, :]], axis=1)
        dr = jnp.concatenate([delta[2 * p : 2 * p + 1, :], delta[2 * p + 1 : 2 * p + 2, :]], axis=1)
        prob = jnp.exp(SCALE * nt(k[:, lanes], qb) - lr)
        ds = (prob * (nt(v[:, lanes], gb) - dr)).astype(BF16)
        dv[p * TOK : (p + 1) * TOK, :] = nn(prob.astype(BF16), gb)
        dk[p * TOK : (p + 1) * TOK, :] = SCALE * nn(ds, qb)
        dq = SCALE * tn(k[:, lanes], ds)
        parts = []
        for e in range(2):
            h = 2 * p + e
            rows = slice(h * HEAD_DIM, (h + 1) * HEAD_DIM)
            total = dq[e * HEAD_DIM : (e + 1) * HEAD_DIM, e * TOK : (e + 1) * TOK]
            for t, x in zip(taken, (s1, s2, s3)):
                total = total + jnp.where(t[h : h + 1], x[rows], 0.0)
            parts.append(total)
        grad_q[:, lanes] = jnp.concatenate(parts, axis=0).T.astype(BF16)


def near_key_body(kv, qg0, qg1, qg2, qg3, st0, st1, st2, st3, dk_near, dv_near):
    refs = (qg0, qg1, qg2, qg3)
    stats = jnp.concatenate([st[:, 0:NEAR] for st in (st0, st1, st2, st3)], axis=1)
    head = iota((2 * NEAR, TOK), 0) < NEAR
    first = iota((NEAR, LANES), 1) < HEAD_DIM
    for p in range(PAIRS):
        lanes = slice(p * LANES, (p + 1) * LANES)
        h = 2 * p
        queries = near_pair(refs, 0, lanes)
        grads = near_pair(refs, 1, lanes)
        lr = jnp.where(head, stats[h : h + 1], stats[h + 1 : h + 2])
        dr = jnp.where(head, stats[16 + h : 17 + h], stats[17 + h : 18 + h])
        prob = jnp.exp(SCALE * nt(pair_block(kv[0:NEAR, lanes]), queries) - lr)
        ds = (prob * (nt(pair_block(kv[NEAR : 2 * NEAR, lanes]), grads) - dr)).astype(BF16)
        dk = nn(ds, queries)
        dv = nn(prob.astype(BF16), grads)
        dk_near[:, lanes] = SCALE * jnp.where(first, dk[0:NEAR], dk[NEAR:])
        dv_near[:, lanes] = jnp.where(first, dv[0:NEAR], dv[NEAR:])


def stat_pick(slots):
    columns = heads_of(slots) * slots
    bits = slots.bit_length() - 1
    return one_hot(
        (iota((WIDTH, columns), 0) & 255) >> 4 == iota((WIDTH, columns), 1) >> bits
    )


def far_expand(line, pick):
    slot = iota((1, FAR_SLOT, WIDTH), 1)
    mask = ((iota((1, FAR_SLOT, WIDTH), 2) & 15) == slot + MID) & (slot < FAR)
    x = jnp.where(mask, line[:, None, :], 0.0).reshape(line.shape[0] * FAR_SLOT, WIDTH)
    return nn(x.astype(BF16), pick)


def far_key_grad(qg, key, value, lse, delta):
    s, dp = far_products(qg, key, value)
    valid = in_slots(s.shape[0], FAR_SLOT, 0, FAR, s.shape[1])
    prob = jnp.exp(jnp.where(valid, s - lse, NEGATIVE))
    ds = jnp.where(valid, prob * (dp - delta), 0.0).astype(BF16)
    dk = SCALE * head_sum(tn(ds, qg), 8)
    dv = head_sum(tn(pltpu.roll(prob, FAR, 0).astype(BF16), qg), 8)
    return dk, dv


def mid_key_grad(queries, grads, key, value, lse, delta):
    prob = jnp.exp(SCALE * nt(queries, head_block(key, 16)) - lse)
    ds = (prob * (nt(grads, head_block(value, 16)) - delta)).astype(BF16)
    return SCALE * head_sum(tn(ds, queries), 16), head_sum(tn(prob.astype(BF16), grads), 16)


def key_grad_body(off, place, dk0, dv0, dk1, dv1, far_a, far_b, own, *rest):
    mids, (grad_k_hbm, grad_v_hbm, grad_k, grad_v, sems) = rest[:8], rest[8:]
    far = jnp.concatenate([far_a[...], far_b[...]], axis=0)
    own32 = own[...].astype(F32)
    line = iota((64, 2 * CHIPS * FAR_SLOT), 0)
    chip = (line & 15) ^ place[0]
    source = ((line >> 4) & 1) * (CHIPS * FAR_SLOT) + chip * FAR_SLOT + 6 + (line >> 5)
    lines2 = nn(one_hot(iota(line.shape, 1) == source), far)
    lines3 = far.astype(F32).reshape(2 * CHIPS, FAR_SLOT, WIDTH)
    device = iota((TOK, 32), 1) * MID
    row = iota((TOK, 32), 0)
    spread = one_hot((row >= device) & (row < device + MID))
    slot = lax.rem(iota((TOK, 1), 0), MID)
    mask = (iota((TOK, WIDTH), 1) & 15) == slot
    lines2 = lines2.astype(BF16)
    pick2 = stat_pick(16)
    lse2, delta2 = (
        nn(jnp.where(mask, nn(spread, lines2[32 * e : 32 * e + 32]), 0.0).astype(BF16), pick2)
        for e in range(2)
    )
    dk2, dv2 = mid_key_grad(stack(mids, 0), stack(mids, 1), own32[0:16], own32[16:32], lse2, delta2)
    pick3 = stat_pick(8)
    lse3 = far_expand(lines3[:, 6, :], pick3)
    delta3 = far_expand(lines3[:, 7, :], pick3)
    dk3, dv3 = far_key_grad(far, own32[64:72], own32[80:88], lse3, delta3)
    token = iota((TOK, WIDTH), 0)
    taken = [(token & (SPANS[b] - 1)) == offset_row(off, b) for b in range(3)]
    outs = []
    for out, hbm, base, one, two, three in (
        (grad_k, grad_k_hbm, dk0, dk1, dk2, dk3),
        (grad_v, grad_v_hbm, dv0, dv1, dv2, dv3),
    ):
        total = jnp.concatenate([base[p * TOK : (p + 1) * TOK, :] for p in range(PAIRS)], axis=1)
        total = total + jnp.where(taken[0], spread_tok(one[...], NEAR, SHIFTS[0]), 0.0)
        total = total + jnp.where(taken[1], spread_tok(two, 16, SHIFTS[1]), 0.0)
        total = total + jnp.where(taken[2], spread_tok(three, 8, SHIFTS[2]), 0.0)
        out[...] = total.astype(BF16)
        outs.append(pltpu.make_async_copy(out, hbm, sems.at[len(outs)]))
        outs[-1].start()
    wait(outs)


def flip(value, mask):
    pairs = [(source, source ^ mask) for source in range(lax.axis_size("seq"))]
    return lax.ppermute(value, "seq", pairs)


def exchange(value, groups):
    return lax.all_to_all(value, "seq", 0, 0, tiled=True, axis_index_groups=groups)


def near_first(value):
    return value, flip(value, 1), flip(value, 2)


def near_direct(value):
    return value, flip(value, 1), flip(value, 2), flip(value, 3)


def near_second(values):
    return tuple(values) + (flip(values[2], 1),)


def near_gather(value):
    return near_second(near_first(value))


def plane_row(block):
    return [block] + [flip(block, d) for d in (8, 16, 24)]


def after(values, *deps):
    held = lax.optimization_barrier((tuple(values), tuple(deps)))
    return held[0]


def on_device(queries, keys, values, grad_out, offsets):
    devices = lax.axis_size("seq")
    chip_groups = [list(range(c, devices, 2)) for c in range(2)]
    place = (lax.axis_index("seq") >> 1).astype(jnp.int32).reshape(1)

    near_kv, near_qg, mid_kvqg, far_rep, far_qg, own, q_in, k_in, v_in = call(
        select_body,
        [
            shape(2 * NEAR, WIDTH, BF16),
            shape(2 * NEAR, WIDTH, BF16),
            shape(2 * MID_SLOT, WIDTH, BF16),
            shape(CHIPS * FAR_SLOT, WIDTH, BF16),
            shape(16, WIDTH, BF16),
            shape(128, WIDTH, BF16),
        ]
        + [shape(TOK, WIDTH, BF16)] * 3,
        [
            pltpu.VMEM((TOK, WIDTH), BF16),
            pltpu.VMEM((4 * PAIRS * TOK + 8, LANES), F32),
            pltpu.VMEM((64, WIDTH), F32),
            pltpu.SemaphoreType.DMA((4, CHUNKS)),
            pltpu.VMEM((4 * NEAR, WIDTH), BF16),
            pltpu.VMEM((CHIPS * FAR_SLOT, WIDTH), BF16),
            pltpu.SemaphoreType.DMA((3,)),
        ],
        5,
        hbm=(1, 2, 3, 4),
        hbm_out=(0, 1, 3),
        held=(0,),
        held_out=(2, 4, 5),
        kept_out=(6, 7, 8),
    )(offsets, queries, keys, values, grad_out)

    far_a = exchange(far_rep, chip_groups)
    lines = [mid_kvqg] + [flip(mid_kvqg, d) for d in (2, 4, 6)]
    near_kvs = near_gather(near_kv)
    parts = [
        jnp.concatenate([x[a * MID : (a + 1) * MID] for x in lines], axis=0) for a in range(4)
    ]
    mid_kv = jnp.concatenate(parts[0:2], axis=0)
    mid_qg = jnp.concatenate(parts[2:4], axis=0)
    mid_kvs = plane_row(mid_kv)

    out0, peak0, total0 = call(
        local_forward_body,
        [shape(WIDTH, TOK, F32), shape(16, TOK, F32), shape(16, TOK, F32)],
        (),
        3,
        (),
        kept=(0, 1, 2),
        kept_out=(0, 1, 2),
    )(q_in, after((k_in,), mid_kv)[0], v_in)
    out1, peak1, total1 = call(
        near_forward_body,
        [shape(WIDTH, LANES, F32), shape(16, LANES, F32), shape(16, LANES, F32)],
        (),
        5,
        (),
        1,
        held=(0, 1, 2, 3, 4),
        kept_out=(0, 1, 2),
    )(after((near_qg,), peak0)[0], *near_kvs)
    near_qgs = near_first(after((near_qg,), mid_kv)[0])
    mid_kvs, near_qgs = after((tuple(mid_kvs), near_qgs), peak1)
    far_a = after((far_a,), *mid_kvs)[0]
    far_b = flip(far_a, 1)
    near_qgs = near_second(near_qgs)
    mid_kvs = list(mid_kvs) + [flip(x, 1) for x in mid_kvs]
    out2, peak2, total2 = call(
        mid_forward_body,
        [shape(16, WIDTH, F32), shape(1, 192, F32), shape(1, 192, F32)],
        (),
        9,
        (),
        held=tuple(range(9)),
        kept_out=(0, 1, 2),
    )(own, *mid_kvs)
    out3, peak3, total3 = call(
        far_forward_body,
        [shape(8, WIDTH, F32), shape(1, 128, F32), shape(1, 128, F32)],
        (),
        3,
        (),
        held=(0, 1, 2),
        kept_out=(0, 1, 2),
    )(far_a, far_b, after((own,), peak2)[0])
    attended, lse, delta, near_stat, far_send = call(
        merge_body,
        [
            shape(TOK, WIDTH, BF16),
            shape(16, TOK, F32),
            shape(16, TOK, F32),
            shape(32, LANES, F32),
            shape(CHIPS * FAR_SLOT, WIDTH, BF16),
        ],
        (),
        15,
        held=(0, 1, 14),
        kept=tuple(range(2, 14)),
        held_out=(0, 3, 4),
        kept_out=(1, 2),
    )(
        offsets, grad_out, out0, peak0, total0, out1, peak1, total1, out2, peak2, total2,
        out3, peak3, total3, far_qg,
    )

    back_a = exchange(far_send, chip_groups)
    mid_qgs = plane_row(after((mid_qg,), lse)[0])
    near_qg = after((near_qg,), lse, *near_qgs)[0]

    grad_q, dk0, dv0 = call(
        local_grad_body,
        [
            shape(TOK, WIDTH, BF16),
            shape(PAIRS * TOK, LANES, F32),
            shape(PAIRS * TOK, LANES, F32),
        ],
        [pltpu.VMEM((WIDTH, LANES), F32)]
        + [pltpu.VMEM((TOK, WIDTH), BF16)] * 4
        + [pltpu.SemaphoreType.DMA((4, CHUNKS))],
        24,
        cost=10,
        held=(0,) + tuple(range(5, 13)) + tuple(range(15, 24)),
        hbm=(1, 2, 3, 4),
        kept=(13, 14),
        held_out=(0,),
        kept_out=(1, 2),
    )(
        offsets, queries, keys, values, grad_out, near_qg, *near_kvs, far_a, far_b, own, lse,
        delta, near_stat, *mid_kvs,
    )
    near_stats = near_direct(after((near_stat,), grad_q)[0])
    mid_qgs = after(mid_qgs, grad_q)
    back_a = after((back_a,), *mid_qgs, *near_stats)[0]
    mid_qgs = list(mid_qgs) + [flip(x, 1) for x in mid_qgs]
    back_b = flip(back_a, 1)
    dk1, dv1 = call(
        near_key_body,
        [shape(NEAR, WIDTH, F32), shape(NEAR, WIDTH, F32)],
        (),
        9,
        (),
        held=tuple(range(9)),
        kept_out=(0, 1),
    )(after((near_kv,), back_a)[0], *near_qgs, *near_stats)
    grad_k, grad_v = call(
        key_grad_body,
        [shape(TOK, WIDTH, BF16), shape(TOK, WIDTH, BF16)],
        [
            pltpu.VMEM((TOK, WIDTH), BF16),
            pltpu.VMEM((TOK, WIDTH), BF16),
            pltpu.SemaphoreType.DMA((2,)),
        ],
        17,
        (0, 1),
        hbm_out=(0, 1),
        held=tuple(range(6, 17)),
        kept=(2, 3, 4, 5),
    )(offsets, place, dk0, dv0, dk1, dv1, back_a, back_b, own, *mid_qgs)
    return attended, grad_q, grad_k, grad_v


def solution(mesh):
    placed = (P("seq", None), P("seq", None), P("seq", None), P("seq", None), P())
    return jax.shard_map(
        on_device,
        mesh=mesh,
        in_specs=placed,
        out_specs=(P("seq", None),) * 4,
        check_vma=False,
    )
```
